512 devices in a mesh: corpus: 128 (over y, z, core), query: 4 (over x).
Axes of the slice: x: 4, y: 4, z: 16, core: 2. Of those that a mesh axis runs over, the one named last changes fastest.
Arguments:
- queries_in: bfloat16 [512, 768], P('query'), may hold values from -6 to 6
- head_weight: bfloat16 [768, 768], replicated, may hold values from -0.21875 to 0.21875
- codebook: bfloat16 [96, 2048], replicated, may hold values from -40 to 40
- codes: int32 [49152, 96], P('corpus'), may hold values from 0 to 255
- slab_sizes: int32 [128], P('corpus'), may hold values from 1 to 384, as said below
- positive_ids: int32 [512], P('query'), may hold values from 0 to 49151, as said below
Outputs:
- query_loss: float32 [512], P('query')
- head_grad: float32 [768, 768], P('query')
- codebook_grad: float32 [96, 2048], replicated
The draws below stay inside these ranges and needn't reach their ends.
Inputs may be any that keep to these rules, and one draw needn't show every extreme that they name: `slab_sizes`: live passages of each slab of 384 slots; one shard's slab is full and another holds one passage. `positive_ids`: each names a live slot, counting the slabs of the corpus shards one after another.
All inputs are finite; a program needn't handle non-finite values.
Results may differ from the reference program's by a relative error of at most 0.0045.
Values may be sent and summed in bfloat16 or wider, within the bound.
A program may use at most 64 MiB of HBM per device.

```python
import jax
import jax.numpy as jnp
from jax import lax

D = 768
M = 96
K = 256
SUB = 8
MEAN_DEV = 128
SLOT_DEV = 384
PASSAGES = 49152
QUERIES = 512


def slab_lengths(key):
    shard_count = PASSAGES // SLOT_DEV
    key_counts, key_heavy = jax.random.split(jax.random.fold_in(key, 101))
    slab_counts = jax.random.randint(key_counts, (shard_count,), 1, 2 * MEAN_DEV + 1)
    heavy_shard = jax.random.randint(key_heavy, (), 0, shard_count)
    shard_index = jnp.arange(shard_count)
    slab_counts = jnp.where(shard_index == heavy_shard, SLOT_DEV, slab_counts)
    slab_counts = jnp.where(shard_index == (heavy_shard + 1) % shard_count, 1, slab_counts)
    return slab_counts.astype(jnp.int32)


def draw_slab_sizes(key, part):
    return slab_lengths(key)


def draw_positive_ids(key, part):
    slab_counts = slab_lengths(key)
    key = jax.random.fold_in(key, 5)
    shard_count = PASSAGES // SLOT_DEV
    key_shard, key_offset = jax.random.split(key)
    pos_shard = jax.random.randint(key_shard, (QUERIES,), 0, shard_count)
    offset = jax.random.randint(key_offset, (QUERIES,), 0, 1 << 20) % slab_counts[pos_shard]
    return (pos_shard * SLOT_DEV + offset).astype(jnp.int32)


def draw_codebook(key, part):
    key = jax.random.fold_in(key, 11)
    key_base = jax.random.fold_in(key, 0)
    values = jnp.clip(jax.random.normal(key_base, (M, K, SUB), jnp.float32) * 0.05, -0.3, 0.3)
    return values.reshape(M, K * SUB).astype(jnp.bfloat16)


def touch_ends(entries, stream_key, low, high):
    shape = entries.shape
    place = [jax.random.randint(jax.random.fold_in(stream_key, axis), (), 0, shape[axis]) for axis in range(len(shape))]
    entries = entries.at[tuple(place)].set(low)
    longest = shape.index(max(shape))
    place[longest] = (place[longest] + 1) % shape[longest]
    return entries.at[tuple(place)].set(high)


def shard_levels(key, dims, pieces, least, high):
    loudness, own = 1.0, jax.random.fold_in(key, 6)
    for axis_at, shards_of in pieces:
        heights = jnp.exp(jax.random.uniform(jax.random.fold_in(own, axis_at), (shards_of,), jnp.float32, least / len(pieces), high / len(pieces)))
        loudness = loudness * jnp.repeat(heights, dims[axis_at] // shards_of).reshape([-1 if axis == axis_at else 1 for axis in range(len(dims))])
    return loudness


def noise(key, shape, width, limit, cuts=(), kind=jnp.bfloat16):
    array = jax.random.normal(key, shape, jnp.float32) * width
    if len(cuts) > 0:
        array = shard_levels(key, shape, cuts, -0.22, 0.18) * array
    return jnp.clip(array, min=-limit, max=limit).astype(kind)


def setup_inputs(seed: int = 0) -> dict:
    seeds = jax.random.split(jax.random.key(seed), 7)
    queries_in = noise(seeds[0], (QUERIES, D), 1.0, 6.0, ((0, 4),))
    head_weight = noise(seeds[1], (D, D), D ** -0.5, 0.21875)
    codebook = draw_codebook(jax.random.fold_in(seeds[6], 71), 0)
    codes = touch_ends(jax.random.randint(seeds[3], (PASSAGES, M), 0, K), jax.random.fold_in(seeds[3], 1), 0, K - 1).astype(jnp.int32)
    slab_sizes = draw_slab_sizes(jax.random.fold_in(seeds[6], 71), 0)
    positive_ids = draw_positive_ids(jax.random.fold_in(seeds[6], 71), 0)
    return dict(queries_in=queries_in, head_weight=head_weight, codebook=codebook, codes=codes, slab_sizes=slab_sizes, positive_ids=positive_ids)


def rebuild_rows(code_rows, centroids):
    picked = centroids[jnp.arange(M)[None, :], code_rows]
    return picked.reshape(code_rows.shape[0], M * SUB)


def reference(queries_in, head_weight, codebook, codes, slab_sizes, positive_ids):
    query_vec = jnp.dot(queries_in, head_weight, preferred_element_type=jnp.float32).astype(jnp.bfloat16)
    centroids = codebook.reshape(M, K, SUB)
    shard_count = PASSAGES // SLOT_DEV
    slabs = codes.reshape(shard_count, SLOT_DEV, M)
    slot_index = jnp.arange(SLOT_DEV)

    def scores_of(slab_codes, length):
        passage_rows = rebuild_rows(slab_codes, centroids)
        scores = jnp.dot(query_vec, passage_rows.T, preferred_element_type=jnp.float32)
        alive = slot_index[None, :] < length
        return passage_rows, jnp.where(alive, scores, -jnp.inf)

    def forward(loop_state, slab_item):
        row_peak, totals = loop_state
        passage_rows, scores = scores_of(slab_item[0], slab_item[1])
        new_peak = jnp.maximum(row_peak, jnp.max(scores, axis=1))
        totals = totals * jnp.exp(row_peak - new_peak) + jnp.sum(jnp.exp(scores - new_peak[:, None]), axis=1)
        return (new_peak, totals), None

    start_peak = jnp.full((QUERIES,), -jnp.inf, jnp.float32)
    start_total = jnp.zeros((QUERIES,), jnp.float32)
    (row_peak, totals), _ = lax.scan(forward, (start_peak, start_total), (slabs, slab_sizes))
    log_total = row_peak + jnp.log(totals)
    pos_codes = codes[positive_ids]
    pos_rows = rebuild_rows(pos_codes, centroids)
    pos_score = jnp.sum(query_vec.astype(jnp.float32) * pos_rows.astype(jnp.float32), axis=1)
    query_loss = log_total - pos_score

    base_index = (jnp.arange(M) * K)[None, :]

    def backward(loop_state, slab_item):
        query_grad, book_grad = loop_state
        passage_rows, scores = scores_of(slab_item[0], slab_item[1])
        soft_probs = jnp.exp(scores - log_total[:, None]).astype(jnp.bfloat16)
        query_grad = query_grad + jnp.dot(soft_probs, passage_rows, preferred_element_type=jnp.float32)
        passage_grad = jnp.dot(soft_probs.T, query_vec, preferred_element_type=jnp.float32)
        segment_ids = (base_index + slab_item[0]).reshape(-1)
        book_grad = book_grad + jax.ops.segment_sum(passage_grad.reshape(-1, SUB), segment_ids, num_segments=M * K)
        return (query_grad, book_grad), None

    start_grads = (jnp.zeros((QUERIES, D), jnp.float32), jnp.zeros((M * K, SUB), jnp.float32))
    (query_grad, book_grad), _ = lax.scan(backward, start_grads, (slabs, slab_sizes))
    query_grad = query_grad - pos_rows.astype(jnp.float32)
    pos_segments = (base_index + pos_codes).reshape(-1)
    book_grad = book_grad - jax.ops.segment_sum(query_vec.astype(jnp.float32).reshape(-1, SUB), pos_segments, num_segments=M * K)
    grad_rounded = query_grad.astype(jnp.bfloat16)
    head_grad = jnp.dot(queries_in.T, grad_rounded, preferred_element_type=jnp.float32)
    return query_loss, head_grad, book_grad.reshape(M, K * SUB)
```

```python
import functools

import jax
import jax.numpy as jnp
from jax import lax
from jax.experimental import pallas as pl
from jax.experimental.pallas import tpu as pltpu
from jax.sharding import PartitionSpec as P

D = 768
M = 96
K = 256
SUB = 8
SLOT_DEV = 384
Q_DEV = 128
LANES = 128
TILES = 6
MESH = pl.DeviceIdType.MESH
NT = (((1,), (1,)), ((), ()))
VMEM_BYTES = 48 * 1024 * 1024


def grid_of(mesh):
    corpus, across = mesh.shape["corpus"], mesh.shape["query"]
    up = {128: 4, 8: 2}[corpus]
    return across, up, corpus // (2 * up)


def place(nz):
    c = lax.axis_index("corpus")
    return lax.axis_index("query"), c // (2 * nz), lax.rem(c // 2, nz), lax.rem(c, 2)


def score_kernel(
    length_ref, qin_ref, weight_ref, cent_ref, codes_ref, ids_ref,
    qt_ref, qint_ref, pt_ref, st_ref, codest_ref, stats_ref,
    codes_i, table_rows,
):
    query = jnp.dot(qin_ref[...], weight_ref[...], preferred_element_type=jnp.float32)
    query = query.astype(jnp.bfloat16)
    qt_ref[...] = query.astype(jnp.float32).T.astype(jnp.bfloat16)
    qint_ref[...] = qin_ref[...].astype(jnp.float32).T.astype(jnp.bfloat16)

    codes = codes_ref[...].astype(jnp.float32)
    codes = jnp.concatenate([codes, jnp.zeros((SLOT_DEV, LANES - M), jnp.float32)], axis=1)
    codes = codes.T
    codest_ref[...] = codes
    codes_i[...] = codes.astype(jnp.int32)

    def rebuild(pair, carry):
        halves = []
        for half in range(2):
            m = pair * 2 + half
            table = cent_ref[pl.ds(pl.multiple_of(m * SUB, SUB), SUB), :]
            row = codes_i[pl.ds(m, 1), :]
            parts = []
            for tile in range(SLOT_DEV // LANES):
                index = jnp.broadcast_to(row[:, tile * LANES : (tile + 1) * LANES], (SUB, LANES))
                low = index & (LANES - 1)
                first = jnp.take_along_axis(table[:, :LANES], low, axis=1, mode="promise_in_bounds")
                second = jnp.take_along_axis(table[:, LANES:], low, axis=1, mode="promise_in_bounds")
                parts.append(jnp.where(index >= LANES, second, first))
            halves.append(jnp.concatenate(parts, axis=1))
        rows = jnp.concatenate(halves, axis=0).astype(jnp.bfloat16)
        pt_ref[pl.ds(pl.multiple_of(pair * 2 * SUB, 2 * SUB), 2 * SUB), :] = rows
        return carry

    lax.fori_loop(0, M // 2, rebuild, 0, unroll=4)
    scores = jnp.dot(query, pt_ref[...], preferred_element_type=jnp.float32).T
    slot = lax.broadcasted_iota(jnp.int32, (SLOT_DEV, Q_DEV), 0)
    scores = jnp.where(slot < length_ref[0], scores, -jnp.inf)
    st_ref[...] = scores
    owned = slot == ids_ref[...] - lax.axis_index("corpus") * SLOT_DEV
    peak = jnp.max(scores, axis=0, keepdims=True)
    total = jnp.sum(jnp.exp(scores - peak), axis=0, keepdims=True)
    positive = jnp.sum(jnp.where(owned, scores, 0.0), axis=0, keepdims=True)
    stats_ref[0:1, :] = peak
    stats_ref[1:2, :] = total
    stats_ref[2:3, :] = positive
    stats_ref[3:8, :] = jnp.zeros((5, Q_DEV), jnp.float32)


def local_scores(length, queries_in, head_weight, cent, codes, ids):
    whole = pl.BlockSpec(memory_space=pltpu.VMEM)
    return pl.pallas_call(
        score_kernel,
        out_shape=[
            jax.ShapeDtypeStruct((D, Q_DEV), jnp.bfloat16),
            jax.ShapeDtypeStruct((D, Q_DEV), jnp.bfloat16),
            jax.ShapeDtypeStruct((D, SLOT_DEV), jnp.bfloat16),
            jax.ShapeDtypeStruct((SLOT_DEV, Q_DEV), jnp.float32),
            jax.ShapeDtypeStruct((LANES, SLOT_DEV), jnp.float32),
            jax.ShapeDtypeStruct((8, Q_DEV), jnp.float32),
        ],
        in_specs=[pl.BlockSpec(memory_space=pltpu.SMEM)] + [whole] * 5,
        out_specs=[whole] * 6,
        scratch_shapes=[
            pltpu.VMEM((LANES, SLOT_DEV), jnp.int32),
            pltpu.VMEM((8, LANES), jnp.float32),
        ],
        compiler_params=pltpu.CompilerParams(vmem_limit_bytes=VMEM_BYTES),
    )(length, queries_in, head_weight, cent, codes, ids)


def merge(slots):
    peaks, totals, positives = slots[:, 0, :], slots[:, 1, :], slots[:, 2, :]
    peak = jnp.max(peaks, axis=0, keepdims=True)
    total = jnp.sum(totals * jnp.exp(peaks - peak), axis=0, keepdims=True)
    return peak, total, jnp.sum(positives, axis=0, keepdims=True)


def totals_kernel(ny, nz, stats_ref, out_ref, near, far, mid, ns, nr, fs, fr):
    x, y, z, core = place(nz)
    group = ny * 2
    me = y * 2 + core

    def near_id(other):
        return {"corpus": ((other // 2) * nz + z) * 2 + lax.rem(other, 2), "query": x}

    def far_id(other):
        return {"corpus": (y * nz + other) * 2 + core, "query": x}

    barrier = pltpu.get_barrier_semaphore()

    def greet_near(d, carry):
        pl.semaphore_signal(barrier, 1, device_id=near_id(lax.rem(me + d, group)), device_id_type=MESH)
        return carry

    def greet_far(d, carry):
        pl.semaphore_signal(barrier, 1, device_id=far_id(lax.rem(z + d, nz)), device_id_type=MESH)
        return carry

    lax.fori_loop(1, group, greet_near, 0)
    lax.fori_loop(1, nz, greet_far, 0)
    pl.semaphore_wait(barrier, group + nz - 2)

    def near_copy(d):
        return pltpu.make_async_remote_copy(
            src_ref=stats_ref, dst_ref=near.at[me], send_sem=ns.at[d], recv_sem=nr.at[d],
            device_id=near_id(lax.rem(me + d, group)), device_id_type=MESH,
        )

    def far_copy(d):
        return pltpu.make_async_remote_copy(
            src_ref=mid, dst_ref=far.at[z], send_sem=fs.at[d], recv_sem=fr.at[d],
            device_id=far_id(lax.rem(z + d, nz)), device_id_type=MESH,
        )

    def loop(count, act):
        def body(d, carry):
            act(d)
            return carry

        lax.fori_loop(1, count, body, 0)

    loop(group, lambda d: near_copy(d).start())
    near[me] = stats_ref[...]
    loop(group, lambda d: near_copy(d).wait_recv())
    peak, total, positive = merge(near[...])
    pad = jnp.zeros((5, Q_DEV), jnp.float32)
    mid[...] = jnp.concatenate([peak, total, positive, pad], axis=0)
    loop(nz, lambda d: far_copy(d).start())
    far[z] = mid[...]
    loop(nz, lambda d: far_copy(d).wait_recv())
    peak, total, positive = merge(far[...])
    log_total = peak + jnp.log(total)
    out_ref[...] = jnp.concatenate([log_total, log_total - positive, positive, pad], axis=0)
    loop(group, lambda d: near_copy(d).wait_send())
    loop(nz, lambda d: far_copy(d).wait_send())


def query_totals(ny, nz, stats):
    whole = pl.BlockSpec(memory_space=pltpu.VMEM)
    dma = pltpu.SemaphoreType.DMA
    return pl.pallas_call(
        functools.partial(totals_kernel, ny, nz),
        out_shape=jax.ShapeDtypeStruct((8, Q_DEV), jnp.float32),
        in_specs=[whole],
        out_specs=whole,
        scratch_shapes=[
            pltpu.VMEM((ny * 2, 8, Q_DEV), jnp.float32),
            pltpu.VMEM((nz, 8, Q_DEV), jnp.float32),
            pltpu.VMEM((8, Q_DEV), jnp.float32),
            dma((ny * 2,)),
            dma((ny * 2,)),
            dma((nz,)),
            dma((nz,)),
        ],
        compiler_params=pltpu.CompilerParams(collective_id=0, has_side_effects=True),
    )(stats)


def grad_kernel(ids_ref, totals_ref, qt_ref, pt_ref, st_ref, codest_ref, grad_ref, book_ref, pgt):
    probs = jnp.exp(st_ref[...] - totals_ref[0:1, :]).astype(jnp.bfloat16)
    slot = lax.broadcasted_iota(jnp.int32, (SLOT_DEV, Q_DEV), 0)
    owned = slot == ids_ref[...] - lax.axis_index("corpus") * SLOT_DEV
    positive = jnp.where(owned, -1.0, 0.0).astype(jnp.bfloat16)
    both = jnp.concatenate([probs, positive], axis=1)
    query = qt_ref[...]
    pgt[...] = lax.dot_general(
        jnp.concatenate([query, query], axis=1), both, NT, preferred_element_type=jnp.float32
    )
    grads = jnp.dot(pt_ref[...], both, preferred_element_type=jnp.float32)
    grad_ref[...] = grads[:, :Q_DEV] + grads[:, Q_DEV:]
    word = lax.broadcasted_iota(jnp.int32, (K, SLOT_DEV), 0).astype(jnp.float32)
    word = word.astype(jnp.bfloat16)

    def scatter(m, carry):
        rows = pl.ds(pl.multiple_of(m * SUB, SUB), SUB)
        grad = pgt[rows, :]
        upper = grad.astype(jnp.bfloat16)
        lower = (grad - upper.astype(jnp.float32)).astype(jnp.bfloat16)
        code = codest_ref[pl.ds(m, 1), :].astype(jnp.bfloat16)
        onehot = jnp.where(word == code, jnp.bfloat16(1), jnp.bfloat16(0))
        halves = lax.dot_general(
            jnp.concatenate([upper, lower], axis=0), onehot, NT, preferred_element_type=jnp.float32
        )
        book_ref[rows, :] = halves[:SUB] + halves[SUB:]
        return carry

    lax.fori_loop(0, M, scatter, 0, unroll=8)


def local_grads(ids, totals, qt, pt, st, codest):
    whole = pl.BlockSpec(memory_space=pltpu.VMEM)
    return pl.pallas_call(
        grad_kernel,
        out_shape=[
            jax.ShapeDtypeStruct((D, Q_DEV), jnp.float32),
            jax.ShapeDtypeStruct((D, K), jnp.float32),
        ],
        in_specs=[whole] * 6,
        out_specs=[whole] * 2,
        scratch_shapes=[pltpu.VMEM((D, SLOT_DEV), jnp.float32)],
        compiler_params=pltpu.CompilerParams(vmem_limit_bytes=VMEM_BYTES),
    )(ids, totals, qt, pt, st, codest)


def sums_kernel(
    nx, ny, nz, grad_ref, book_ref, qint_ref, head_ref, out_ref,
    q_all, g_core, g_send, g_block, g_sum, g_z, g_red, g_fin,
    c_core, c_send, c_block, c_sum, c_z, c_red, c_fin,
    q_sems, gc_sems, gy_sems, gz_send, gz_recv, gr_send, gr_recv, gf_sems, gs_sems,
    cc_sems, cy_sems, cz_send, cz_recv, cr_send, cr_recv, cf_sems, cs_sems,
):
    x, y, z, core = place(nz)
    other = 1 - core
    chips = nx * ny
    here = x * ny + y
    half = D // 2
    head_rows = D // nx
    g_rows = half // ny
    c_rows = half // chips
    g_tile = g_rows // TILES
    c_tile = 2 * c_rows // TILES
    sibling = {"corpus": (y * nz + z) * 2 + other, "query": x}

    def chip(g):
        return {"corpus": (lax.rem(g, ny) * nz + z) * 2 + core, "query": g // ny}

    def far(o):
        return {"corpus": (y * nz + o) * 2 + core, "query": x}

    def copy(src, dst, send, recv, device):
        return pltpu.make_async_remote_copy(
            src_ref=src, dst_ref=dst, send_sem=send, recv_sem=recv, device_id=device, device_id_type=MESH
        )

    def loop(start, count, act):
        def body(d, carry):
            act(d)
            return carry

        lax.fori_loop(start, count, body, 0)

    def at_chip(d):
        return lax.rem(here + d, chips)

    def from_chip(d):
        return lax.rem(here + chips - d, chips)

    def at_y(d):
        return lax.rem(y + d, ny)

    barrier = pltpu.get_barrier_semaphore()
    pl.semaphore_signal(barrier, 1, device_id=sibling, device_id_type=MESH)
    loop(1, chips, lambda d: pl.semaphore_signal(barrier, 1, device_id=chip(at_chip(d)), device_id_type=MESH))
    loop(1, nz, lambda d: pl.semaphore_signal(barrier, 1, device_id=far(lax.rem(z + d, nz)), device_id_type=MESH))
    pl.semaphore_wait(barrier, chips + nz - 1)

    def g_core_copy(d):
        rows = pl.ds(pl.multiple_of(other * half + at_y(d) * g_rows, 8), g_rows)
        return copy(grad_ref.at[rows], g_core.at[d], gc_sems.at[0, d], gc_sems.at[1, d], sibling)

    def c_core_copy(d):
        rows = pl.ds(pl.multiple_of(other * half + at_chip(d) * c_rows, 8), c_rows)
        return copy(book_ref.at[rows], c_core.at[d], cc_sems.at[0, d], cc_sems.at[1, d], sibling)

    def q_copy(d):
        to = lax.rem(x + d, nx)
        rows = pl.ds(pl.multiple_of(to * head_rows, 16), head_rows)
        device = {"corpus": lax.axis_index("corpus"), "query": to}
        return copy(qint_ref.at[rows], q_all.at[x], q_sems.at[0, d], q_sems.at[1, d], device)

    def g_y_copy(d):
        device = {"corpus": (at_y(d) * nz + z) * 2 + core, "query": x}
        return copy(g_send.at[d], g_block.at[d], gy_sems.at[0, d], gy_sems.at[1, d], device)

    def c_chip_copy(d):
        return copy(c_send.at[d], c_block.at[d], cy_sems.at[0, d], cy_sems.at[1, d], chip(at_chip(d)))

    def g_part(t):
        return (pl.ds(t * g_tile, g_tile), slice(None))

    def c_part(t):
        return (pl.ds((t // 2) * c_tile, c_tile), pl.ds((t % 2) * LANES, LANES))

    def g_owner(t):
        return (t * nz) // TILES

    def c_owner(t):
        return ((2 * t + 1) * nz) // (2 * TILES)

    def slot(owner, t):
        return sum(1 for s in range(t) if owner(s) == owner(t))

    def z_copy(t, send, recv, owner, part, z_in, z_send, z_recv):
        return copy(
            send.at[part(t)], z_in.at[slot(owner, t), z], z_send.at[t], z_recv.at[slot(owner, t), z], far(owner(t))
        )

    def z_heard(t, o, owner, z_in, z_send, z_recv):
        tile = z_in.at[slot(owner, t), o]
        return copy(tile, tile, z_send.at[t], z_recv.at[slot(owner, t), o], far(o))

    g_final = g_fin.at[x, core, y]
    c_final = c_fin.at[core, here]

    def scatter_z(total, owner, part, z_in, z_send, z_recv):
        for t in range(TILES):
            mine = z == owner(t)

            @pl.when(mine)
            def _(t=t):
                z_in[slot(owner, t), z] = total[part(t)]

            @pl.when(jnp.logical_not(mine))
            def _(t=t):
                z_copy(t, total, None, owner, part, z_in, z_send, z_recv).start()

    def reduced_copy(t, d, owner, part, red, final, send, recv):
        return copy(
            red.at[slot(owner, t)], final.at[part(t)], send.at[slot(owner, t), d], recv.at[t],
            far(lax.rem(z + d, nz)),
        )

    def reduce_z(owner, part, z_in, z_send, z_recv, red, final, send, recv, dtype):
        for t in range(TILES):

            @pl.when(z == owner(t))
            def _(t=t):
                loop(1, nz, lambda d: z_heard(t, lax.rem(z + d, nz), owner, z_in, z_send, z_recv).wait_recv())
                whole = jnp.sum(z_in[slot(owner, t)], axis=0).astype(dtype)
                red[slot(owner, t)] = whole
                loop(1, nz, lambda d: reduced_copy(t, d, owner, part, red, final, send, recv).start())
                final[part(t)] = whole

    def heard_z(owner, part, red, final, send, recv):
        for t in range(TILES):

            @pl.when(z != owner(t))
            def _(t=t):
                reduced_copy(t, 0, owner, part, red, final, send, recv).wait_recv()

    def sent_z(total, owner, part, z_in, z_send, z_recv, red, final, send, recv):
        for t in range(TILES):
            mine = z == owner(t)

            @pl.when(mine)
            def _(t=t):
                loop(1, nz, lambda d: reduced_copy(t, d, owner, part, red, final, send, recv).wait_send())

            @pl.when(jnp.logical_not(mine))
            def _(t=t):
                z_copy(t, total, None, owner, part, z_in, z_send, z_recv).wait_send()

    def g_out(d):
        return copy(g_final, g_final, gf_sems.at[0, d], gf_sems.at[1, d], chip(at_chip(d)))

    def g_in(d):
        there = from_chip(d)
        block = g_fin.at[there // ny, core, lax.rem(there, ny)]
        return copy(block, block, gf_sems.at[0, d], gf_sems.at[1, d], chip(there))

    def g_share(d):
        there = from_chip(d)
        block = g_fin.at[there // ny, core, lax.rem(there, ny)]
        return copy(block, block, gs_sems.at[0, d], gs_sems.at[1, d], sibling)

    def g_shared(d):
        there = from_chip(d)
        block = g_fin.at[there // ny, other, lax.rem(there, ny)]
        return copy(block, block, gs_sems.at[0, d], gs_sems.at[1, d], sibling)

    def c_out(d):
        return copy(c_final, c_final, cf_sems.at[0, d], cf_sems.at[1, d], chip(at_chip(d)))

    def c_in(d):
        block = c_fin.at[core, from_chip(d)]
        return copy(block, block, cf_sems.at[0, d], cf_sems.at[1, d], chip(from_chip(d)))

    def c_share(d):
        block = c_fin.at[core, from_chip(d)]
        return copy(block, block, cs_sems.at[0, d], cs_sems.at[1, d], sibling)

    def c_shared(d):
        block = c_fin.at[other, from_chip(d)]
        return copy(block, block, cs_sems.at[0, d], cs_sems.at[1, d], sibling)

    loop(1, ny, lambda d: g_core_copy(d).start())
    g_core_copy(0).start()
    loop(1, chips, lambda d: c_core_copy(d).start())
    c_core_copy(0).start()
    loop(1, nx, lambda d: q_copy(d).start())
    q_all[x] = qint_ref[pl.ds(pl.multiple_of(x * head_rows, 16), head_rows), :]

    def g_forward(d):
        g_core_copy(d).wait_recv()
        rows = pl.ds(pl.multiple_of(core * half + at_y(d) * g_rows, 8), g_rows)
        g_send[d] = grad_ref[rows, :] + g_core[d]

    def g_go(d):
        g_forward(d)
        g_y_copy(d).start()

    def c_forward(d):
        c_core_copy(d).wait_recv()
        rows = pl.ds(pl.multiple_of(core * half + at_chip(d) * c_rows, 8), c_rows)
        c_send[d] = book_ref[rows, :] + c_core[d]

    def c_go(d):
        c_forward(d)
        c_chip_copy(d).start()

    loop(1, ny, g_go)
    g_forward(0)
    loop(1, chips, c_go)
    c_forward(0)

    g_args = (g_owner, g_part, g_z, gz_send, gz_recv)
    c_args = (c_owner, c_part, c_z, cz_send, cz_recv)
    g_more = (g_red, g_final, gr_send, gr_recv)
    c_more = (c_red, c_final, cr_send, cr_recv)
    loop(1, ny, lambda d: g_y_copy(d).wait_recv())
    total = g_send[0]
    for d in range(1, ny):
        total = total + g_block[d]
    g_sum[...] = total
    scatter_z(g_sum, *g_args)
    loop(1, chips, lambda d: c_chip_copy(d).wait_recv())
    total = c_send[0]
    for d in range(1, chips):
        total = total + c_block[d]
    c_sum[...] = total
    scatter_z(c_sum, *c_args)
    reduce_z(*g_args, *g_more, jnp.bfloat16)
    reduce_z(*c_args, *c_more, jnp.float32)

    heard_z(g_owner, g_part, *g_more)
    loop(1, chips, lambda d: g_out(d).start())
    g_share(0).start()
    heard_z(c_owner, c_part, *c_more)
    loop(1, chips, lambda d: c_out(d).start())
    c_share(0).start()

    def g_pass(d):
        g_in(d).wait_recv()
        g_share(d).start()

    def c_pass(d):
        c_in(d).wait_recv()
        c_share(d).start()

    loop(1, chips, g_pass)
    loop(1, chips, c_pass)
    loop(0, chips, lambda d: g_shared(d).wait_recv())
    loop(1, nx, lambda d: q_copy(d).wait_recv())
    head = jnp.zeros((head_rows, D), jnp.float32)
    for o in range(nx):
        head = head + lax.dot_general(
            q_all[o], g_fin[o].reshape(D, Q_DEV), NT, preferred_element_type=jnp.float32
        )
    head_ref[...] = head
    loop(0, chips, lambda d: c_shared(d).wait_recv())
    out_ref[...] = c_fin[...].reshape(D, K)

    loop(0, ny, lambda d: g_core_copy(d).wait_send())
    loop(0, chips, lambda d: c_core_copy(d).wait_send())
    loop(1, nx, lambda d: q_copy(d).wait_send())
    loop(1, ny, lambda d: g_y_copy(d).wait_send())
    loop(1, chips, lambda d: c_chip_copy(d).wait_send())
    sent_z(g_sum, *g_args, *g_more)
    sent_z(c_sum, *c_args, *c_more)
    loop(1, chips, lambda d: g_out(d).wait_send())
    loop(0, chips, lambda d: g_share(d).wait_send())
    loop(1, chips, lambda d: c_out(d).wait_send())
    loop(0, chips, lambda d: c_share(d).wait_send())


def device_sums(nx, ny, nz, grad, book, qint):
    whole = pl.BlockSpec(memory_space=pltpu.VMEM)
    dma = pltpu.SemaphoreType.DMA
    f32, bf16 = jnp.float32, jnp.bfloat16
    chips = nx * ny
    per = -(-TILES // nz)
    g_rows, c_rows = D // 2 // ny, D // 2 // chips
    g_tile, c_tile = g_rows // TILES, 2 * c_rows // TILES
    return pl.pallas_call(
        functools.partial(sums_kernel, nx, ny, nz),
        out_shape=[
            jax.ShapeDtypeStruct((D // nx, D), f32),
            jax.ShapeDtypeStruct((D, K), f32),
        ],
        in_specs=[whole] * 3,
        out_specs=[whole] * 2,
        scratch_shapes=[
            pltpu.VMEM((nx, D // nx, Q_DEV), bf16),
            pltpu.VMEM((ny, g_rows, Q_DEV), f32),
            pltpu.VMEM((ny, g_rows, Q_DEV), f32),
            pltpu.VMEM((ny, g_rows, Q_DEV), f32),
            pltpu.VMEM((g_rows, Q_DEV), f32),
            pltpu.VMEM((per, nz, g_tile, LANES), f32),
            pltpu.VMEM((per, g_tile, LANES), bf16),
            pltpu.VMEM((nx, 2, ny, g_rows, Q_DEV), bf16),
            pltpu.VMEM((chips, c_rows, K), f32),
            pltpu.VMEM((chips, c_rows, K), f32),
            pltpu.VMEM((chips, c_rows, K), f32),
            pltpu.VMEM((c_rows, K), f32),
            pltpu.VMEM((per, nz, c_tile, LANES), f32),
            pltpu.VMEM((per, c_tile, LANES), f32),
            pltpu.VMEM((2, chips, c_rows, K), f32),
            dma((2, nx)),
            dma((2, ny)),
            dma((2, ny)),
            dma((TILES,)),
            dma((per, nz)),
            dma((per, nz)),
            dma((TILES,)),
            dma((2, chips)),
            dma((2, chips)),
            dma((2, chips)),
            dma((2, chips)),
            dma((TILES,)),
            dma((per, nz)),
            dma((per, nz)),
            dma((TILES,)),
            dma((2, chips)),
            dma((2, chips)),
        ],
        compiler_params=pltpu.CompilerParams(
            collective_id=1, has_side_effects=True, vmem_limit_bytes=VMEM_BYTES
        ),
    )(grad, book, qint)


def shards(sizes, queries_in, head_weight, codebook, codes, slab_sizes, positive_ids):
    nx, ny, nz = sizes
    cent = codebook.reshape(M, K, SUB).transpose(0, 2, 1).reshape(D, K).astype(jnp.float32)
    ids = positive_ids.reshape(1, Q_DEV)
    qt, qint, pt, st, codest, stats = local_scores(slab_sizes, queries_in, head_weight, cent, codes, ids)
    totals = query_totals(ny, nz, stats)
    grad, book = local_grads(ids, totals, qt, pt, st, codest)
    head_grad, book = device_sums(nx, ny, nz, grad, book, qint)
    flat_book = book.reshape(M, SUB, K).transpose(0, 2, 1).reshape(M, K * SUB)
    return (totals[1], head_grad, flat_book)


def solution(mesh):
    return jax.shard_map(
        functools.partial(shards, grid_of(mesh)),
        mesh=mesh,
        in_specs=(P("query", None), P(), P(), P("corpus", None), P("corpus"), P("query")),
        out_specs=(P("query"), P("query", None), P()),
        check_vma=False,
    )
```

```python
import functools

import jax
import jax.numpy as jnp
from jax import lax
from jax.experimental import pallas as pl
from jax.experimental.pallas import tpu as pltpu
from jax.sharding import PartitionSpec as P

D = 768
M = 96
K = 256
SUB = 8
SLOT_DEV = 384
Q_DEV = 128
LANES = 128
NX = 4
NY = 4
CHIPS = NX * NY
HALF = D // 2
G_ROWS = HALF // NY
C_ROWS = HALF // CHIPS
C_SUBS = C_ROWS // SUB
HEAD_ROWS = D // NX
TILES = 6
G_TILE = G_ROWS // TILES
LAG = 3
NEAR = 2 * NY
MESH = pl.DeviceIdType.MESH
NT = (((1,), (1,)), ((), ()))
VMEM_BYTES = 64 * 1024 * 1024 - 65536


def loop(start, count, act):
    def body(step, carry):
        act(step)
        return carry

    lax.fori_loop(start, count, body, 0)


def spread(a):
    return 2 - a + 3 * (a // 2) - 2 * (a // 3)


def step_kernel(
    nz,
    length_ref, ids_hbm, qin_hbm, weight_hbm, codebook_hbm, codes_hbm,
    loss_ref, head_ref, out_ref,
    ids, qin, weight, codebook, codes, table, pt, qt, qint, pgt, stats, near, far, mid, book, grad,
    q_all, g_core, g_send, g_block, g_sum, g_z, g_red, g_fin,
    c_core, c_send, c_block, c_sum, c_z, c_red, c_fin,
    in_sems, near_sems, far_sems,
    q_sems, gc_sems, gy_sems, gz_send, gz_recv, gr_send, gr_recv, gf_sems, gs_sems,
    cc_sems, cy_sems, cz_send, cz_recv, cr_send, cr_recv, cf_sems, cs_sems,
):
    me = lax.axis_index("corpus")
    x, y, z, core = lax.axis_index("query"), me // (2 * nz), lax.rem(me // 2, nz), lax.rem(me, 2)
    other = 1 - core
    group = y * 2 + core

    def device(to_x, to_y, to_z, to_core):
        return {"corpus": (to_y * nz + to_z) * 2 + to_core, "query": to_x}

    sibling = device(x, y, z, other)

    def around(o):
        return device(x, o // 2, z, lax.rem(o, 2))

    def along(o):
        return device(x, y, o, core)

    def hop(e):
        return nz // 2 + ((e + 1) // 2) * (1 - 2 * lax.rem(e, 2))

    def chip_at(s, sign):
        to_x = lax.rem(x + 4 + sign * spread(s // 4), NX)
        to_y = lax.rem(y + 4 + sign * spread(lax.rem(s, 4)), NY)
        return to_x, to_y

    def place_at(s, sign):
        to_x, to_y = chip_at(s, sign)
        return to_x * NY + to_y

    def chip(s, sign=1):
        to_x, to_y = chip_at(s, sign)
        return device(to_x, to_y, z, core)

    def y_at(d):
        return lax.rem(y + d, NY)

    def copy(src, dst, send, recv, to):
        return pltpu.make_async_remote_copy(
            src_ref=src, dst_ref=dst, send_sem=send, recv_sem=recv, device_id=to, device_id_type=MESH
        )

    loads = [
        pltpu.make_async_copy(src, dst, in_sems.at[i])
        for i, (src, dst) in enumerate(
            [(codebook_hbm, codebook), (codes_hbm, codes), (qin_hbm, qin), (weight_hbm, weight), (ids_hbm, ids)]
        )
    ]
    for load in loads:
        load.start()
    barrier = pltpu.get_barrier_semaphore()

    def greet(to):
        pl.semaphore_signal(barrier, 1, device_id=to, device_id_type=MESH)

    loop(0, nz - 1, lambda e: greet(along(lax.rem(z + hop(e), nz))))
    loop(1, NEAR, lambda d: greet(around(lax.rem(group + d, NEAR))))
    loop(0, 12, lambda s: greet(chip(s)))

    loads[0].wait()
    wide = K * SUB // 2
    down = lax.broadcasted_iota(jnp.int32, (wide, wide), 0)
    across = lax.broadcasted_iota(jnp.int32, (wide, wide), 1)
    pick = down == (across % LANES) * SUB + across // LANES
    pick = jnp.where(pick, jnp.float32(1), jnp.float32(0)).astype(jnp.bfloat16)
    for part in range(2):
        words = jnp.dot(
            codebook[:, part * wide : (part + 1) * wide], pick, preferred_element_type=jnp.float32
        )
        for j in range(SUB):
            table[pl.ds(part * D + j, M, stride=SUB), :] = words[:, j * LANES : (j + 1) * LANES]
    loads[1].wait()

    def rebuild(pair, carry):
        halves = []
        for part in range(2):
            m = pair * 2 + part
            lower = table[pl.ds(pl.multiple_of(m * SUB, SUB), SUB), :]
            upper = table[pl.ds(pl.multiple_of(D + m * SUB, SUB), SUB), :]
            row = codes[pl.ds(m, 1), :]
            parts = []
            for tile in range(SLOT_DEV // LANES):
                index = jnp.broadcast_to(row[:, tile * LANES : (tile + 1) * LANES], (SUB, LANES))
                low = index & (LANES - 1)
                first = jnp.take_along_axis(lower, low, axis=1, mode="promise_in_bounds")
                second = jnp.take_along_axis(upper, low, axis=1, mode="promise_in_bounds")
                parts.append(jnp.where(index >= LANES, second, first))
            halves.append(jnp.concatenate(parts, axis=1))
        rows = jnp.concatenate(halves, axis=0).astype(jnp.bfloat16)
        pt[pl.ds(pl.multiple_of(pair * 2 * SUB, 2 * SUB), 2 * SUB), :] = rows
        return carry

    lax.fori_loop(0, M // 2, rebuild, 0, unroll=4)

    loads[2].wait()
    loads[3].wait()
    loads[4].wait()
    query = jnp.dot(qin[...], weight[...], preferred_element_type=jnp.float32).astype(jnp.bfloat16)
    scores = jnp.dot(query, pt[...], preferred_element_type=jnp.float32).T
    slot = lax.broadcasted_iota(jnp.int32, (SLOT_DEV, Q_DEV), 0)
    scores = jnp.where(slot < length_ref[0], scores, -jnp.inf)
    owned = slot == ids[...] - me * SLOT_DEV
    peak = jnp.max(scores, axis=0, keepdims=True)
    total = jnp.sum(jnp.exp(scores - peak), axis=0, keepdims=True)
    positive = jnp.sum(jnp.where(owned, scores, 0.0), axis=0, keepdims=True)
    pad = jnp.zeros((5, Q_DEV), jnp.float32)
    stats[...] = jnp.concatenate([peak, total, positive, pad], axis=0)
    pl.semaphore_wait(barrier, NEAR - 1 + nz - 1 + 12)

    def merge(slots):
        peaks, totals, positives = slots[:, 0, :], slots[:, 1, :], slots[:, 2, :]
        peak = jnp.max(peaks, axis=0, keepdims=True)
        total = jnp.sum(totals * jnp.exp(peaks - peak), axis=0, keepdims=True)
        return peak, total, jnp.sum(positives, axis=0, keepdims=True)

    def near_copy(d):
        to = around(lax.rem(group + d, NEAR))
        return copy(stats, near.at[group], near_sems.at[0, d], near_sems.at[1, d], to)

    def far_copy(e):
        to = along(lax.rem(z + hop(e), nz))
        return copy(mid, far.at[z], far_sems.at[0, e], far_sems.at[1, e], to)

    def q_copy(d):
        to = lax.rem(x + d, NX)
        rows = pl.ds(pl.multiple_of(to * HEAD_ROWS, 16), HEAD_ROWS)
        return copy(qint.at[rows], q_all.at[x], q_sems.at[0, d], q_sems.at[1, d], device(to, y, z, core))

    loop(1, NEAR, lambda d: near_copy(d).start())
    near[group] = stats[...]
    qt[...] = query.astype(jnp.float32).T.astype(jnp.bfloat16)
    qint[...] = qin[...].astype(jnp.float32).T.astype(jnp.bfloat16)
    loop(1, NEAR, lambda d: near_copy(d).wait_recv())
    mid[...] = jnp.concatenate([*merge(near[...]), pad], axis=0)
    loop(0, nz - 1, lambda e: far_copy(e).start())
    far[z] = mid[...]
    loop(1, NX, lambda d: q_copy(d).start())
    q_all[x] = qint[pl.ds(pl.multiple_of(x * HEAD_ROWS, 16), HEAD_ROWS), :]
    loop(0, nz - 1, lambda e: far_copy(e).wait_recv())
    peak, total, positive = merge(far[...])
    log_total = peak + jnp.log(total)
    loss_ref[...] = log_total - positive

    probs = jnp.exp(scores - log_total).astype(jnp.bfloat16)
    both = jnp.concatenate([probs, jnp.where(owned, -1.0, 0.0).astype(jnp.bfloat16)], axis=1)
    sides = jnp.dot(pt[...], both, preferred_element_type=jnp.float32)
    grad[...] = sides[:, :Q_DEV] + sides[:, Q_DEV:]

    def g_core_copy(d):
        rows = pl.ds(pl.multiple_of(other * HALF + y_at(d) * G_ROWS, 8), G_ROWS)
        return copy(grad.at[rows], g_core.at[d], gc_sems.at[0, d], gc_sems.at[1, d], sibling)

    loop(0, NY, lambda d: g_core_copy(lax.rem(d + 1, NY)).start())
    twice = jnp.concatenate([qt[...], qt[...]], axis=1)
    pgt[...] = lax.dot_general(twice, both, NT, preferred_element_type=jnp.float32)
    word = lax.broadcasted_iota(jnp.int32, (K, SLOT_DEV), 0).astype(jnp.float32)
    word = word.astype(jnp.bfloat16)

    def scatter(m):
        rows = pl.ds(pl.multiple_of(m * SUB, SUB), SUB)
        part = pgt[rows, :]
        upper = part.astype(jnp.bfloat16)
        lower = (part - upper.astype(jnp.float32)).astype(jnp.bfloat16)
        code = codes[pl.ds(m, 1), :].astype(jnp.float32).astype(jnp.bfloat16)
        onehot = jnp.where(word == code, jnp.bfloat16(1), jnp.bfloat16(0))
        halves = lax.dot_general(
            jnp.concatenate([upper, lower], axis=0), onehot, NT, preferred_element_type=jnp.float32
        )
        book[rows, :] = halves[:SUB] + halves[SUB:]

    def c_rows(s, side):
        return pl.ds(pl.multiple_of(side * HALF + place_at(s, 1) * C_ROWS, 8), C_ROWS)

    def c_core_copy(s):
        return copy(
            book.at[c_rows(s, other)], c_core.at[s], cc_sems.at[0, s], cc_sems.at[1, s], sibling
        )

    def c_chip_copy(s):
        return copy(c_send.at[s], c_block.at[s], cy_sems.at[0, s], cy_sems.at[1, s], chip(s))

    def c_compute(s):
        for side in (other, core):
            first = side * (M // 2) + place_at(s, 1) * C_SUBS
            for i in range(C_SUBS):
                scatter(first + i)
            if side is other:
                c_core_copy(s).start()

    def c_finish(s):
        c_core_copy(s).wait_recv()
        c_send[s] = book[c_rows(s, core), :] + c_core[s]

    def c_go(s):
        c_finish(s)
        c_chip_copy(s).start()

    def c_both(s):
        c_compute(s)
        c_go(s - LAG)

    def g_y_copy(d):
        return copy(g_send.at[d], g_block.at[d], gy_sems.at[0, d], gy_sems.at[1, d], device(x, y_at(d), z, core))

    def g_finish(d):
        g_core_copy(d).wait_recv()
        rows = pl.ds(pl.multiple_of(core * HALF + y_at(d) * G_ROWS, 8), G_ROWS)
        g_send[d] = grad[rows, :] + g_core[d]

    def g_go(d):
        g_finish(d)
        g_y_copy(d).start()

    def g_part(t):
        return (pl.ds(t * G_TILE, G_TILE), slice(None))

    def c_part(t):
        return (pl.ds((t // 2) * SUB, SUB), pl.ds((t % 2) * LANES, LANES))

    def c_out_part(t):
        return (pl.ds(t * SUB, SUB), slice(None))

    def g_owner(t):
        return (t * nz) // TILES

    def c_owner(t):
        return ((2 * t + 1) * nz) // (2 * TILES)

    def place(owner, t):
        return sum(1 for s in range(t) if owner(s) == owner(t))

    def z_copy(t, total, owner, part, z_in, z_send, z_recv):
        p = place(owner, t)
        return copy(total.at[part(t)], z_in.at[p, z], z_send.at[t], z_recv.at[p, z], along(owner(t)))

    def z_heard(t, o, owner, z_in, z_send, z_recv):
        p = place(owner, t)
        return copy(z_in.at[p, o], z_in.at[p, o], z_send.at[t], z_recv.at[p, o], along(o))

    def scatter_z(total, owner, part, z_in, z_send, z_recv):
        for t in range(TILES):
            mine = z == owner(t)

            @pl.when(mine)
            def _(t=t):
                z_in[place(owner, t), z] = total[part(t)]

            @pl.when(jnp.logical_not(mine))
            def _(t=t):
                z_copy(t, total, owner, part, z_in, z_send, z_recv).start()

    def back_copy(t, e, owner, part, red, final, send, recv):
        p = place(owner, t)
        to = along(lax.rem(z + hop(e), nz))
        return copy(red.at[p], final.at[part(t)], send.at[p, e], recv.at[t], to)

    def reduce_z(shape, owner, z_in, z_send, z_recv, part, red, final, send, recv):
        for t in range(TILES):

            @pl.when(z == owner(t))
            def _(t=t):
                loop(
                    0, nz - 1,
                    lambda e: z_heard(t, lax.rem(z + hop(e), nz), owner, z_in, z_send, z_recv).wait_recv(),
                )
                whole = shape(jnp.sum(z_in[place(owner, t)], axis=0))
                red[place(owner, t)] = whole
                loop(0, nz - 1, lambda e: back_copy(t, e, owner, part, red, final, send, recv).start())
                final[part(t)] = whole

    def heard_z(owner, part, red, final, send, recv):
        for t in range(TILES):

            @pl.when(z != owner(t))
            def _(t=t):
                back_copy(t, 0, owner, part, red, final, send, recv).wait_recv()

    def sent_z(total, owner, part, z_in, z_send, z_recv, out_part, red, final, send, recv):
        for t in range(TILES):
            mine = z == owner(t)

            @pl.when(mine)
            def _(t=t):
                loop(0, nz - 1, lambda e: back_copy(t, e, owner, out_part, red, final, send, recv).wait_send())

            @pl.when(jnp.logical_not(mine))
            def _(t=t):
                z_copy(t, total, owner, part, z_in, z_send, z_recv).wait_send()

    def interleave(tile):
        down = lax.broadcasted_iota(jnp.int32, (SUB, LANES), 0)
        across = lax.broadcasted_iota(jnp.int32, (SUB, LANES), 1)
        index = down * (LANES // SUB) + across // SUB
        mixed = jnp.zeros((SUB, LANES), jnp.float32)
        for j in range(SUB):
            row = jnp.broadcast_to(tile[j : j + 1, :], (SUB, LANES))
            row = jnp.take_along_axis(row, index, axis=1, mode="promise_in_bounds")
            mixed = jnp.where(across % SUB == j, row, mixed)
        return mixed

    loop(0, LAG, c_compute)
    loop(1, NY, g_go)
    g_finish(0)
    loop(LAG, 10, c_both)
    loop(1, NY, lambda d: g_y_copy(d).wait_recv())
    g_total = g_send[0]
    for d in range(1, NY):
        g_total = g_total + g_block[d]
    g_sum[...] = g_total
    g_final = g_fin.at[x, core, y]
    g_way = (g_owner, g_part, g_z, gz_send, gz_recv)
    g_back = (g_red, g_final, gr_send, gr_recv)
    scatter_z(g_sum, *g_way)
    loop(10, CHIPS, c_both)
    loop(CHIPS - LAG, CHIPS - 1, c_go)
    c_finish(CHIPS - 1)

    loop(0, CHIPS - 1, lambda s: c_chip_copy(s).wait_recv())
    c_total = c_send[CHIPS - 1]
    for s in range(CHIPS - 1):
        c_total = c_total + c_block[s]
    c_sum[...] = c_total

    def c_final_at(side, place):
        return c_fin.at[pl.ds(pl.multiple_of((side * CHIPS + place) * 2 * C_ROWS, 8), 2 * C_ROWS)]

    c_final = c_final_at(core, x * NY + y)
    c_way = (c_owner, c_part, c_z, cz_send, cz_recv)
    c_back = (c_red, c_final, cr_send, cr_recv)
    scatter_z(c_sum, *c_way)
    reduce_z(lambda a: a.astype(jnp.bfloat16), g_owner, *g_way[2:], g_part, *g_back)
    reduce_z(interleave, c_owner, *c_way[2:], c_out_part, *c_back)

    def g_at(side, s):
        from_x, from_y = chip_at(s, -1)
        return g_fin.at[from_x, side, from_y]

    def g_out(s):
        return copy(g_final, g_final, gf_sems.at[0, s], gf_sems.at[1, s], chip(s))

    def g_in(s):
        return copy(g_at(core, s), g_at(core, s), gf_sems.at[0, s], gf_sems.at[1, s], chip(s))

    def g_share(s):
        return copy(g_at(core, s), g_at(core, s), gs_sems.at[0, s], gs_sems.at[1, s], sibling)

    def g_shared(s):
        return copy(g_at(other, s), g_at(other, s), gs_sems.at[0, s], gs_sems.at[1, s], sibling)

    def c_out(s):
        return copy(c_final, c_final, cf_sems.at[0, s], cf_sems.at[1, s], chip(s))

    def c_at(side, s):
        return c_final_at(side, place_at(s, -1))

    def c_in(s):
        return copy(c_at(core, s), c_at(core, s), cf_sems.at[0, s], cf_sems.at[1, s], chip(s))

    def c_share(s):
        return copy(c_at(core, s), c_at(core, s), cs_sems.at[0, s], cs_sems.at[1, s], sibling)

    def c_shared(s):
        return copy(c_at(other, s), c_at(other, s), cs_sems.at[0, s], cs_sems.at[1, s], sibling)

    heard_z(g_owner, g_part, *g_back)
    loop(0, CHIPS - 1, lambda s: g_out(s).start())
    g_share(CHIPS - 1).start()
    heard_z(c_owner, c_out_part, *c_back)
    loop(0, CHIPS - 1, lambda s: c_out(s).start())
    c_share(CHIPS - 1).start()

    def g_pass(s):
        g_in(s).wait_recv()
        g_share(s).start()

    def c_pass(s):
        c_in(s).wait_recv()
        c_share(s).start()

    loop(0, CHIPS - 1, g_pass)
    loop(0, CHIPS, lambda s: g_shared(s).wait_recv())
    loop(1, NX, lambda d: q_copy(d).wait_recv())
    head = jnp.zeros((HEAD_ROWS, D), jnp.float32)
    for o in range(NX):
        head = head + lax.dot_general(
            q_all[o], g_fin[o].reshape(D, Q_DEV), NT, preferred_element_type=jnp.float32
        )
    head_ref[...] = head
    loop(0, CHIPS - 1, c_pass)
    loop(0, CHIPS, lambda s: c_shared(s).wait_recv())
    for u in range(2 * SUB):
        out_ref[:, u * LANES : (u + 1) * LANES] = c_fin[pl.ds(u, M, stride=2 * SUB), :]

    loop(1, NEAR, lambda d: near_copy(d).wait_send())
    loop(0, nz - 1, lambda e: far_copy(e).wait_send())
    loop(1, NX, lambda d: q_copy(d).wait_send())
    loop(0, NY, lambda d: g_core_copy(d).wait_send())
    loop(0, CHIPS, lambda s: c_core_copy(s).wait_send())
    loop(1, NY, lambda d: g_y_copy(d).wait_send())
    loop(0, CHIPS - 1, lambda s: c_chip_copy(s).wait_send())
    sent_z(g_sum, *g_way, g_part, *g_back)
    sent_z(c_sum, *c_way, c_out_part, *c_back)
    loop(0, CHIPS - 1, lambda s: g_out(s).wait_send())
    loop(0, CHIPS, lambda s: g_share(s).wait_send())
    loop(0, CHIPS - 1, lambda s: c_out(s).wait_send())
    loop(0, CHIPS, lambda s: c_share(s).wait_send())


def step(nz, queries_in, head_weight, codebook, codes, slab_sizes, positive_ids):
    whole = pl.BlockSpec(memory_space=pltpu.VMEM)
    left = pl.BlockSpec(memory_space=pltpu.HBM)
    dma = pltpu.SemaphoreType.DMA
    f32, bf16 = jnp.float32, jnp.bfloat16
    per = -(-TILES // nz)
    loss, head_grad, book = pl.pallas_call(
        functools.partial(step_kernel, nz),
        out_shape=[
            jax.ShapeDtypeStruct((1, Q_DEV), f32),
            jax.ShapeDtypeStruct((HEAD_ROWS, D), f32),
            jax.ShapeDtypeStruct((M, K * SUB), f32),
        ],
        in_specs=[pl.BlockSpec(memory_space=pltpu.SMEM)] + [left] * 5,
        out_specs=[whole] * 3,
        scratch_shapes=[
            pltpu.VMEM((1, Q_DEV), jnp.int32),
            pltpu.VMEM((Q_DEV, D), bf16),
            pltpu.VMEM((D, D), bf16),
            pltpu.VMEM((M, K * SUB), bf16),
            pltpu.VMEM((M, SLOT_DEV), jnp.int32),
            pltpu.VMEM((2 * D, LANES), f32),
            pltpu.VMEM((D, SLOT_DEV), bf16),
            pltpu.VMEM((D, Q_DEV), bf16),
            pltpu.VMEM((D, Q_DEV), bf16),
            pltpu.VMEM((D, SLOT_DEV), f32),
            pltpu.VMEM((8, Q_DEV), f32),
            pltpu.VMEM((NEAR, 8, Q_DEV), f32),
            pltpu.VMEM((nz, 8, Q_DEV), f32),
            pltpu.VMEM((8, Q_DEV), f32),
            pltpu.VMEM((D, K), f32),
            pltpu.VMEM((D, Q_DEV), f32),
            pltpu.VMEM((NX, HEAD_ROWS, Q_DEV), bf16),
            pltpu.VMEM((NY, G_ROWS, Q_DEV), f32),
            pltpu.VMEM((NY, G_ROWS, Q_DEV), f32),
            pltpu.VMEM((NY, G_ROWS, Q_DEV), f32),
            pltpu.VMEM((G_ROWS, Q_DEV), f32),
            pltpu.VMEM((per, nz, G_TILE, LANES), f32),
            pltpu.VMEM((per, G_TILE, LANES), bf16),
            pltpu.VMEM((NX, 2, NY, G_ROWS, Q_DEV), bf16),
            pltpu.VMEM((CHIPS, C_ROWS, K), f32),
            pltpu.VMEM((CHIPS, C_ROWS, K), f32),
            pltpu.VMEM((CHIPS, C_ROWS, K), f32),
            pltpu.VMEM((C_ROWS, K), f32),
            pltpu.VMEM((per, nz, SUB, LANES), f32),
            pltpu.VMEM((per, SUB, LANES), f32),
            pltpu.VMEM((2 * D, LANES), f32),
            dma((5,)),
            dma((2, NEAR)),
            dma((2, nz)),
            dma((2, NX)),
            dma((2, NY)),
            dma((2, NY)),
            dma((TILES,)),
            dma((per, nz)),
            dma((per, nz)),
            dma((TILES,)),
            dma((2, CHIPS)),
            dma((2, CHIPS)),
            dma((2, CHIPS)),
            dma((2, CHIPS)),
            dma((TILES,)),
            dma((per, nz)),
            dma((per, nz)),
            dma((TILES,)),
            dma((2, CHIPS)),
            dma((2, CHIPS)),
        ],
        compiler_params=pltpu.CompilerParams(
            collective_id=0, has_side_effects=True, vmem_limit_bytes=VMEM_BYTES
        ),
    )(slab_sizes, positive_ids.reshape(1, Q_DEV), queries_in, head_weight, codebook, codes.T)
    return loss.reshape(Q_DEV), head_grad, book


def solution(mesh):
    nz = mesh.shape["corpus"] // (2 * NY)
    return jax.shard_map(
        functools.partial(step, nz),
        mesh=mesh,
        in_specs=(P("query", None), P(), P(), P("corpus", None), P("corpus"), P("query")),
        out_specs=(P("query"), P("query", None), P()),
        check_vma=False,
    )
```

```python
import functools

import jax
import jax.numpy as jnp
from jax import lax
from jax.experimental import pallas as pl
from jax.experimental.pallas import tpu as pltpu
from jax.sharding import PartitionSpec as P

D = 768
M = 96
K = 256
SUB = 8
SLOT_DEV = 384
Q_DEV = 128
LANES = 128
NX = 4
NY = 4
CHIPS = NX * NY
HALF = D // 2
G_ROWS = HALF // NY
C_ROWS = HALF // CHIPS
C_SUBS = C_ROWS // SUB
HEAD_ROWS = D // NX
TILES = 6
G_TILE = G_ROWS // TILES
NEAR = 2 * NY
MESH = pl.DeviceIdType.MESH
NT = (((1,), (1,)), ((), ()))
VMEM_BYTES = 64 * 1024 * 1024 - 65536


def loop(start, count, act):
    def body(step, carry):
        act(step)
        return carry

    lax.fori_loop(start, count, body, 0)


def spread(a):
    return 2 - a + 3 * (a // 2) - 2 * (a // 3)


def step_kernel(
    nz,
    length_ref, ids_hbm, qin_hbm, weight_hbm, codebook_hbm, codes_hbm,
    loss_hbm, head_hbm, out_hbm,
    ids, qin, weight, codebook, codes, table, pt, qt, qint, pgt, stats, near, far, mid, book,
    pu, sides, mass, fixed, scaled, loss, head, out,
    q_all, grad, g_core, g_send, g_block, g_sum, g_z, g_red, g_fin,
    c_core, c_send, c_block, c_sum, c_pair, c_half, c_many, c_fin,
    in_sems, out_sems, near_sems, far_sems,
    q_sems, gc_sems, gy_sems, gz_send, gz_recv, gr_send, gr_recv, gf_sems, gs_sems,
    cc_sems, cy_sems, cp_sems, cz_sems, cb_sems, cf_sems, cs_sems,
):
    me = lax.axis_index("corpus")
    x, y, z, core = lax.axis_index("query"), me // (2 * nz), lax.rem(me // 2, nz), lax.rem(me, 2)
    other = 1 - core
    group = y * 2 + core

    def device(to_x, to_y, to_z, to_core):
        return {"corpus": (to_y * nz + to_z) * 2 + to_core, "query": to_x}

    sibling = device(x, y, z, other)

    def around(o):
        return device(x, o // 2, z, lax.rem(o, 2))

    def along(o):
        return device(x, y, o, core)

    def hop(e, ring=nz):
        return ring // 2 + ((e + 1) // 2) * (1 - 2 * lax.rem(e, 2))

    def chip_at(s, sign):
        to_x = lax.rem(x + 4 + sign * spread(s // 4), NX)
        to_y = lax.rem(y + 4 + sign * spread(lax.rem(s, 4)), NY)
        return to_x, to_y

    def place_at(s, sign):
        to_x, to_y = chip_at(s, sign)
        return to_x * NY + to_y

    def chip(s, sign=1):
        to_x, to_y = chip_at(s, sign)
        return device(to_x, to_y, z, core)

    def y_at(d):
        return lax.rem(y + d, NY)

    def copy(src, dst, send, recv, to):
        return pltpu.make_async_remote_copy(
            src_ref=src, dst_ref=dst, send_sem=send, recv_sem=recv, device_id=to, device_id_type=MESH
        )

    barrier = pltpu.get_barrier_semaphore()

    def greet(to):
        pl.semaphore_signal(barrier, 1, device_id=to, device_id_type=MESH)

    loop(0, nz - 1, lambda e: greet(along(lax.rem(z + hop(e), nz))))
    loads = [
        pltpu.make_async_copy(src, dst, in_sems.at[i])
        for i, (src, dst) in enumerate(
            [(codebook_hbm, codebook), (codes_hbm, codes), (qin_hbm, qin), (weight_hbm, weight), (ids_hbm, ids)]
        )
    ]
    for load in loads:
        load.start()
    loop(1, NEAR, lambda d: greet(around(lax.rem(group + d, NEAR))))
    loop(0, 12, lambda s: greet(chip(s)))

    wide = K * SUB // 2
    down = lax.broadcasted_iota(jnp.int32, (wide, wide), 0)
    across = lax.broadcasted_iota(jnp.int32, (wide, wide), 1)
    pick = down == (across % LANES) * SUB + across // LANES
    pick = jnp.where(pick, jnp.float32(1), jnp.float32(0)).astype(jnp.bfloat16)
    loads[0].wait()
    for part in range(2):
        words = jnp.dot(
            codebook[:, part * wide : (part + 1) * wide], pick, preferred_element_type=jnp.float32
        )
        for j in range(SUB):
            table[pl.ds(part * D + j, M, stride=SUB), :] = words[:, j * LANES : (j + 1) * LANES]
    loads[1].wait()

    def rebuild(pair, carry):
        halves = []
        for part in range(2):
            m = pair * 2 + part
            lower = table[pl.ds(pl.multiple_of(m * SUB, SUB), SUB), :]
            upper = table[pl.ds(pl.multiple_of(D + m * SUB, SUB), SUB), :]
            row = codes[pl.ds(m, 1), :]
            parts = []
            for tile in range(SLOT_DEV // LANES):
                index = jnp.broadcast_to(row[:, tile * LANES : (tile + 1) * LANES], (SUB, LANES))
                low = index & (LANES - 1)
                first = jnp.take_along_axis(lower, low, axis=1, mode="promise_in_bounds")
                second = jnp.take_along_axis(upper, low, axis=1, mode="promise_in_bounds")
                parts.append(jnp.where(index >= LANES, second, first))
            halves.append(jnp.concatenate(parts, axis=1))
        rows = jnp.concatenate(halves, axis=0).astype(jnp.bfloat16)
        pt[pl.ds(pl.multiple_of(pair * 2 * SUB, 2 * SUB), 2 * SUB), :] = rows
        return carry

    lax.fori_loop(0, M // 2, rebuild, 0, unroll=4)

    loads[2].wait()
    loads[3].wait()
    loads[4].wait()
    query = jnp.dot(qin[...], weight[...], preferred_element_type=jnp.float32).astype(jnp.bfloat16)
    scores = jnp.dot(query, pt[...], preferred_element_type=jnp.float32).T
    slot = lax.broadcasted_iota(jnp.int32, (SLOT_DEV, Q_DEV), 0)
    scores = jnp.where(slot < length_ref[0], scores, -jnp.inf)
    owned = slot == ids[...] - me * SLOT_DEV
    peak = jnp.max(scores, axis=0, keepdims=True)
    raised = jnp.exp(scores - peak)
    total = jnp.sum(raised, axis=0, keepdims=True)
    positive = jnp.sum(jnp.where(owned, scores, 0.0), axis=0, keepdims=True)
    pad = jnp.zeros((5, Q_DEV), jnp.float32)
    stats[...] = jnp.concatenate([peak, total, positive, pad], axis=0)
    pl.semaphore_wait(barrier, NEAR - 1 + nz - 1 + 12)

    def merge(slots):
        peaks, totals, positives = slots[:, 0, :], slots[:, 1, :], slots[:, 2, :]
        peak = jnp.max(peaks, axis=0, keepdims=True)
        total = jnp.sum(totals * jnp.exp(peaks - peak), axis=0, keepdims=True)
        return peak, total, jnp.sum(positives, axis=0, keepdims=True)

    def near_copy(d):
        to = around(lax.rem(group + d, NEAR))
        return copy(stats, near.at[group], near_sems.at[0, d], near_sems.at[1, d], to)

    def far_copy(e):
        to = along(lax.rem(z + hop(e), nz))
        return copy(mid, far.at[z], far_sems.at[0, e], far_sems.at[1, e], to)

    def q_copy(d):
        to = lax.rem(x + d, NX)
        rows = pl.ds(pl.multiple_of(to * HEAD_ROWS, 16), HEAD_ROWS)
        return copy(qint.at[rows], q_all.at[x], q_sems.at[0, d], q_sems.at[1, d], device(to, y, z, core))

    def onto(m):
        rows = pl.ds(pl.multiple_of(m * SUB, SUB), SUB)
        part = pgt[rows, :]
        upper = part.astype(jnp.bfloat16)
        lower = (part - upper.astype(jnp.float32)).astype(jnp.bfloat16)
        code = codes[pl.ds(m, 1), :].astype(jnp.float32).astype(jnp.bfloat16)
        onehot = jnp.where(word == code, jnp.bfloat16(1), jnp.bfloat16(0))
        left = jnp.concatenate([pu[...], upper, lower], axis=0)
        sums = lax.dot_general(left, onehot, NT, preferred_element_type=jnp.float32)
        mass[pl.ds(pl.multiple_of(m * Q_DEV, Q_DEV), Q_DEV), :] = sums[:Q_DEV].astype(jnp.bfloat16)
        fixed[rows, :] = sums[Q_DEV : Q_DEV + SUB] + sums[Q_DEV + SUB :]

    def onto_range(first, last):
        def body(m, carry):
            onto(m)
            return carry

        lax.fori_loop(first, last, body, 0, unroll=4)

    def g_core_copy():
        rows = pl.ds(other * (HALF // 16), HALF // 16)
        return copy(grad.at[rows], g_core, gc_sems.at[0], gc_sems.at[1], sibling)

    def g_y_copy(d):
        to = device(x, y_at(d), z, core)
        return copy(g_send.at[d], g_block.at[d], gy_sems.at[0, d], gy_sems.at[1, d], to)

    def g_pair(d):
        first = y_at(d) * TILES
        mine = grad[pl.ds(core * (HALF // 16) + first, TILES)].astype(jnp.float32)
        return mine + g_core[pl.ds(first, TILES)].astype(jnp.float32)

    def g_go(d):
        g_send[d] = g_pair(d).astype(jnp.bfloat16)
        g_y_copy(d).start()

    loop(1, NEAR, lambda d: near_copy(d).start())
    near[group] = stats[...]
    qt[...] = query.astype(jnp.float32).T.astype(jnp.bfloat16)
    qint[...] = qin[...].astype(jnp.float32).T.astype(jnp.bfloat16)
    pu[...] = raised.T.astype(jnp.bfloat16)
    minus = jnp.where(owned, -1.0, 0.0).astype(jnp.bfloat16)
    both = jnp.concatenate([raised.astype(jnp.bfloat16), minus], axis=1)
    sides[...] = jnp.dot(pt[...], both, preferred_element_type=jnp.float32)
    pgt[...] = lax.dot_general(qt[...], minus, NT, preferred_element_type=jnp.float32)
    word = lax.broadcasted_iota(jnp.int32, (K, SLOT_DEV), 0).astype(jnp.float32)
    word = word.astype(jnp.bfloat16)
    onto_range(0, 12)
    loop(1, NEAR, lambda d: near_copy(d).wait_recv())
    near_peak, near_total, near_positive = merge(near[...])
    mid[...] = jnp.concatenate([near_peak, near_total, near_positive, pad], axis=0)
    loop(0, nz - 1, lambda e: far_copy(e).start())
    far[z] = mid[...]

    tiles = (D // 16, 16, Q_DEV)
    soft = sides[:, :Q_DEV] * jnp.exp(peak - near_peak)
    grad[:, 0] = soft.astype(jnp.bfloat16).reshape(tiles)
    grad[:, 1] = sides[:, Q_DEV:].astype(jnp.bfloat16).reshape(tiles)
    g_core_copy().start()
    loop(1, NX, lambda d: q_copy(d).start())
    q_all[x] = qint[pl.ds(pl.multiple_of(x * HEAD_ROWS, 16), HEAD_ROWS), :]
    onto_range(12, 24)
    g_core_copy().wait_recv()
    loop(1, NY, g_go)
    onto_range(24, 72)

    def g_part(t):
        return (pl.ds(t * G_TILE, G_TILE), slice(None))

    def g_owner(t):
        return (t * nz) // TILES

    def g_place(t):
        return sum(1 for s in range(t) if g_owner(s) == g_owner(t))

    def z_copy(t):
        p = g_place(t)
        return copy(g_sum.at[t], g_z.at[p, z], gz_send.at[t], gz_recv.at[p, z], along(g_owner(t)))

    def z_heard(t, o):
        p = g_place(t)
        return copy(g_z.at[p, o], g_z.at[p, o], gz_send.at[t], gz_recv.at[p, o], along(o))

    g_final = g_fin.at[x, core, y]

    def back_copy(t, e):
        to = along(lax.rem(z + hop(e), nz))
        return copy(g_red.at[g_place(t)], g_final.at[g_part(t)], gr_send.at[g_place(t), e], gr_recv.at[t], to)

    loop(1, NY, lambda d: g_y_copy(d).wait_recv())
    g_total = g_pair(0)
    for d in range(1, NY):
        g_total = g_total + g_block[d].astype(jnp.float32)
    g_sum[...] = g_total.astype(jnp.bfloat16)
    for t in range(TILES):

        @pl.when(z == g_owner(t))
        def _(t=t):
            g_z[g_place(t), z] = g_sum[t]

        @pl.when(z != g_owner(t))
        def _(t=t):
            z_copy(t).start()

    onto_range(72, M)
    loop(0, nz - 1, lambda e: far_copy(e).wait_recv())
    last_peak, total, positive = merge(far[...])
    log_total = last_peak + jnp.log(total)
    loss[...] = log_total - positive
    loss_out = pltpu.make_async_copy(loss, loss_hbm, out_sems.at[0])
    loss_out.start()
    scaled[...] = qt[...].astype(jnp.float32) * jnp.exp(peak - log_total)

    def split(m):
        part = scaled[pl.ds(pl.multiple_of(m * SUB, SUB), SUB), :]
        upper = part.astype(jnp.bfloat16)
        lower = (part - upper.astype(jnp.float32)).astype(jnp.bfloat16)
        return jnp.concatenate([upper, lower], axis=0)

    def mass_of(m):
        return mass[pl.ds(pl.multiple_of(m * Q_DEV, Q_DEV), Q_DEV), :]

    def x_at(a, sign=1):
        return lax.rem(x + 4 + sign * spread(a), NX)

    def c_compute(a):
        for i in range(NY * C_SUBS):
            m0 = other * (M // 2) + x_at(a) * (NY * C_SUBS) + i
            m1 = core * (M // 2) + x_at(a) * (NY * C_SUBS) + i
            nil = jnp.zeros((2 * SUB, Q_DEV), jnp.bfloat16)
            first = jnp.concatenate([split(m0), nil], axis=1)
            second = jnp.concatenate([nil, split(m1)], axis=1)
            sums = jnp.dot(
                jnp.concatenate([first, second], axis=0),
                jnp.concatenate([mass_of(m0), mass_of(m1)], axis=0),
                preferred_element_type=jnp.float32,
            )
            for at, m in ((0, m0), (2 * SUB, m1)):
                rows = pl.ds(pl.multiple_of(m * SUB, SUB), SUB)
                book[rows, :] = sums[at : at + SUB] + sums[at + SUB : at + 2 * SUB] + fixed[rows, :]
        c_core_copy(a).start()

    def c_core_copy(a):
        rows = pl.ds(pl.multiple_of(other * HALF + x_at(a) * NY * C_ROWS, 8), NY * C_ROWS)
        return copy(book.at[rows], c_core.at[a], cc_sems.at[0, a], cc_sems.at[1, a], sibling)

    def c_chip_copy(s):
        return copy(c_send.at[s], c_block.at[s], cy_sems.at[0, s], cy_sems.at[1, s], chip(s))

    def c_add(s):
        to_x, to_y = chip_at(s, 1)
        rows = pl.ds(pl.multiple_of(core * HALF + (to_x * NY + to_y) * C_ROWS, 8), C_ROWS)
        there = pl.ds(pl.multiple_of(to_y * C_ROWS, 8), C_ROWS)
        c_send[s] = book[rows, :] + c_core[s // NY, there, :]

    def c_go(s):
        c_add(s)
        c_chip_copy(s).start()

    def c_forward(a, count):
        c_core_copy(a).wait_recv()
        loop(a * NY, a * NY + count, c_go)

    def c_both(a):
        c_compute(a)
        c_forward(a - 1, NY)

    c_compute(0)
    loop(1, NX, c_both)
    c_forward(NX - 1, NY - 1)
    c_add(CHIPS - 1)

    for t in range(TILES):

        @pl.when(z == g_owner(t))
        def _(t=t):
            loop(0, nz - 1, lambda e: z_heard(t, lax.rem(z + hop(e), nz)).wait_recv())
            weights = jnp.exp(far[...][:, 0, :] - log_total)
            whole = jnp.zeros((16, Q_DEV), jnp.float32)
            for o in range(nz):
                whole = whole + g_z[g_place(t), o, 0].astype(jnp.float32) * weights[o : o + 1, :]
                whole = whole + g_z[g_place(t), o, 1].astype(jnp.float32)
            g_red[g_place(t)] = whole.astype(jnp.bfloat16)
            loop(0, nz - 1, lambda e: back_copy(t, e).start())
            g_final[g_part(t)] = whole.astype(jnp.bfloat16)

    def interleave(tile):
        down = lax.broadcasted_iota(jnp.int32, (SUB, LANES), 0)
        across = lax.broadcasted_iota(jnp.int32, (SUB, LANES), 1)
        index = down * (LANES // SUB) + across // SUB
        mixed = jnp.zeros((SUB, LANES), jnp.float32)
        for j in range(SUB):
            row = jnp.broadcast_to(tile[j : j + 1, :], (SUB, LANES))
            row = jnp.take_along_axis(row, index, axis=1, mode="promise_in_bounds")
            mixed = jnp.where(across % SUB == j, row, mixed)
        return mixed

    loop(0, CHIPS - 1, lambda s: c_chip_copy(s).wait_recv())
    c_total = c_send[CHIPS - 1]
    for s in range(CHIPS - 1):
        c_total = c_total + c_block[s]
    for i in range(C_SUBS):
        for part in range(2):
            tile = c_total[i * SUB : (i + 1) * SUB, part * LANES : (part + 1) * LANES]
            c_sum[pl.ds((2 * i + part) * SUB, SUB), :] = tile

    odd, pair, pairs = lax.rem(z, 2), z // 2, nz // 2
    mate = along(z + 1 - 2 * odd)

    def half_at(which):
        return pl.ds(pl.multiple_of(which * C_ROWS, 8), C_ROWS)

    def c_pair_copy():
        return copy(c_sum.at[half_at(1 - odd)], c_pair, cp_sems.at[0], cp_sems.at[1], mate)

    def c_many_copy(e):
        to = along(lax.rem(pair + hop(e, pairs), pairs) * 2 + odd)
        return copy(c_half, c_many.at[pair], cz_sems.at[0, e], cz_sems.at[1, e], to)

    c_pair_copy().start()

    def c_final_at(side, place):
        return c_fin.at[pl.ds(pl.multiple_of((side * CHIPS + place) * 2 * C_ROWS, 8), 2 * C_ROWS)]

    c_final = c_final_at(core, x * NY + y)
    def g_at(side, s):
        from_x, from_y = chip_at(s, -1)
        return g_fin.at[from_x, side, from_y]

    def g_out(s):
        return copy(g_final, g_final, gf_sems.at[0, s], gf_sems.at[1, s], chip(s))

    def g_in(s):
        return copy(g_at(core, s), g_at(core, s), gf_sems.at[0, s], gf_sems.at[1, s], chip(s))

    def g_row(side, a):
        return g_fin.at[x_at(a, -1), side]

    def g_share(a):
        return copy(g_row(core, a), g_row(core, a), gs_sems.at[0, a], gs_sems.at[1, a], sibling)

    def g_shared(a):
        return copy(g_row(other, a), g_row(other, a), gs_sems.at[0, a], gs_sems.at[1, a], sibling)

    def c_out(s):
        return copy(c_final, c_final, cf_sems.at[0, s], cf_sems.at[1, s], chip(s))

    def c_at(side, s):
        return c_final_at(side, place_at(s, -1))

    def c_in(s):
        return copy(c_at(core, s), c_at(core, s), cf_sems.at[0, s], cf_sems.at[1, s], chip(s))

    def c_row(side, a):
        first = (side * CHIPS + x_at(a, -1) * NY) * 2 * C_ROWS
        return c_fin.at[pl.ds(pl.multiple_of(first, 8), NY * 2 * C_ROWS)]

    def c_share(a):
        return copy(c_row(core, a), c_row(core, a), cs_sems.at[0, a], cs_sems.at[1, a], sibling)

    def c_shared(a):
        return copy(c_row(other, a), c_row(other, a), cs_sems.at[0, a], cs_sems.at[1, a], sibling)

    c_pair_copy().wait_recv()
    c_kept = c_sum[half_at(odd), :] + c_pair[...]
    c_half[...] = c_kept
    c_many[pair] = c_kept
    loop(0, pairs - 1, lambda e: c_many_copy(e).start())
    for t in range(TILES):

        @pl.when(z != g_owner(t))
        def _(t=t):
            back_copy(t, 0).wait_recv()

    loop(0, CHIPS - 1, lambda s: g_out(s).start())
    loop(0, pairs - 1, lambda e: c_many_copy(e).wait_recv())
    c_total = c_many[0]
    for o in range(1, pairs):
        c_total = c_total + c_many[o]
    first = pl.multiple_of(odd * C_ROWS, 8)
    for i in range(C_SUBS):
        c_final[pl.ds(pl.multiple_of(first + i * SUB, 8), SUB), :] = interleave(
            c_total[i * SUB : (i + 1) * SUB]
        )

    def c_back_copy():
        return copy(c_final.at[half_at(odd)], c_final.at[half_at(odd)], cb_sems.at[0], cb_sems.at[1], mate)

    c_back_copy().start()
    c_back_copy().wait_recv()
    loop(0, CHIPS - 1, lambda s: c_out(s).start())

    def pass_on(came, share):
        def act(a):
            loop(a * NY, lax.min(a * NY + NY, CHIPS - 1), lambda s: came(s).wait_recv())
            share(a).start()

        loop(0, NX, act)

    pass_on(g_in, g_share)
    loop(1, NX, lambda d: q_copy(d).wait_recv())
    loop(0, NX, lambda a: g_shared(a).wait_recv())
    total = jnp.zeros((HEAD_ROWS, D), jnp.float32)
    for o in range(NX):
        total = total + lax.dot_general(
            q_all[o], g_fin[o].reshape(D, Q_DEV), NT, preferred_element_type=jnp.float32
        )
    head[...] = total
    head_out = pltpu.make_async_copy(head, head_hbm, out_sems.at[1])
    head_out.start()
    pass_on(c_in, c_share)
    loop(0, NX, lambda a: c_shared(a).wait_recv())
    for u in range(2 * SUB):
        out[:, u * LANES : (u + 1) * LANES] = c_fin[pl.ds(u, M, stride=2 * SUB), :]
    book_out = pltpu.make_async_copy(out, out_hbm, out_sems.at[2])
    book_out.start()

    loop(1, NEAR, lambda d: near_copy(d).wait_send())
    loop(0, nz - 1, lambda e: far_copy(e).wait_send())
    loop(1, NX, lambda d: q_copy(d).wait_send())
    g_core_copy().wait_send()
    loop(0, NX, lambda a: c_core_copy(a).wait_send())
    loop(1, NY, lambda d: g_y_copy(d).wait_send())
    loop(0, CHIPS - 1, lambda s: c_chip_copy(s).wait_send())
    for t in range(TILES):

        @pl.when(z == g_owner(t))
        def _(t=t):
            loop(0, nz - 1, lambda e: back_copy(t, e).wait_send())

        @pl.when(z != g_owner(t))
        def _(t=t):
            z_copy(t).wait_send()

    c_pair_copy().wait_send()
    loop(0, pairs - 1, lambda e: c_many_copy(e).wait_send())
    c_back_copy().wait_send()
    loop(0, CHIPS - 1, lambda s: g_out(s).wait_send())
    loop(0, NX, lambda a: g_share(a).wait_send())
    loop(0, CHIPS - 1, lambda s: c_out(s).wait_send())
    loop(0, NX, lambda a: c_share(a).wait_send())
    loss_out.wait()
    head_out.wait()
    book_out.wait()


def finish_kernel(loss_in, head_in, book_in, loss_out, head_out, book_out, loss, head, book, sems):
    moves = [(loss_in, loss, loss_out)]
    for i in range(2):
        rows = pl.ds(i * (HEAD_ROWS // 2), HEAD_ROWS // 2)
        moves.append((head_in.at[rows], head.at[rows], head_out.at[rows]))
    for i in range(3):
        rows = pl.ds(i * (M // 3), M // 3)
        moves.append((book_in.at[rows], book.at[rows], book_out.at[rows]))
    ins = [pltpu.make_async_copy(src, mid, sems.at[0, i]) for i, (src, mid, _) in enumerate(moves)]
    outs = [pltpu.make_async_copy(mid, dst, sems.at[1, i]) for i, (_, mid, dst) in enumerate(moves)]
    for each in ins:
        each.start()
    for one, two in zip(ins, outs):
        one.wait()
        two.start()
    for each in outs:
        each.wait()


def step(nz, queries_in, head_weight, codebook, codes, slab_sizes, positive_ids):
    left = pl.BlockSpec(memory_space=pltpu.HBM)
    dma = pltpu.SemaphoreType.DMA
    f32, bf16 = jnp.float32, jnp.bfloat16
    per = -(-TILES // nz)
    loss, head_grad, book = pl.pallas_call(
        functools.partial(step_kernel, nz),
        out_shape=[
            jax.ShapeDtypeStruct((1, Q_DEV), f32),
            jax.ShapeDtypeStruct((HEAD_ROWS, D), f32),
            jax.ShapeDtypeStruct((M, K * SUB), f32),
        ],
        in_specs=[pl.BlockSpec(memory_space=pltpu.SMEM)] + [left] * 5,
        out_specs=[left] * 3,
        scratch_shapes=[
            pltpu.VMEM((1, Q_DEV), jnp.int32),
            pltpu.VMEM((Q_DEV, D), bf16),
            pltpu.VMEM((D, D), bf16),
            pltpu.VMEM((M, K * SUB), bf16),
            pltpu.VMEM((M, SLOT_DEV), jnp.int32),
            pltpu.VMEM((2 * D, LANES), f32),
            pltpu.VMEM((D, SLOT_DEV), bf16),
            pltpu.VMEM((D, Q_DEV), bf16),
            pltpu.VMEM((D, Q_DEV), bf16),
            pltpu.VMEM((D, SLOT_DEV), f32),
            pltpu.VMEM((8, Q_DEV), f32),
            pltpu.VMEM((NEAR, 8, Q_DEV), f32),
            pltpu.VMEM((nz, 8, Q_DEV), f32),
            pltpu.VMEM((8, Q_DEV), f32),
            pltpu.VMEM((D, K), f32),
            pltpu.VMEM((Q_DEV, SLOT_DEV), bf16),
            pltpu.VMEM((D, 2 * Q_DEV), f32),
            pltpu.VMEM((M * Q_DEV, K), bf16),
            pltpu.VMEM((D, K), f32),
            pltpu.VMEM((D, Q_DEV), f32),
            pltpu.VMEM((1, Q_DEV), f32),
            pltpu.VMEM((HEAD_ROWS, D), f32),
            pltpu.VMEM((M, K * SUB), f32),
            pltpu.VMEM((NX, HEAD_ROWS, Q_DEV), bf16),
            pltpu.VMEM((D // 16, 2, 16, Q_DEV), bf16),
            pltpu.VMEM((HALF // 16, 2, 16, Q_DEV), bf16),
            pltpu.VMEM((NY, TILES, 2, 16, Q_DEV), bf16),
            pltpu.VMEM((NY, TILES, 2, 16, Q_DEV), bf16),
            pltpu.VMEM((TILES, 2, 16, Q_DEV), bf16),
            pltpu.VMEM((per, nz, 2, 16, Q_DEV), bf16),
            pltpu.VMEM((per, 16, Q_DEV), bf16),
            pltpu.VMEM((NX, 2, NY, G_ROWS, Q_DEV), bf16),
            pltpu.VMEM((NX, NY * C_ROWS, K), f32),
            pltpu.VMEM((CHIPS, C_ROWS, K), f32),
            pltpu.VMEM((CHIPS, C_ROWS, K), f32),
            pltpu.VMEM((2 * C_ROWS, LANES), f32),
            pltpu.VMEM((C_ROWS, LANES), f32),
            pltpu.VMEM((C_ROWS, LANES), f32),
            pltpu.VMEM((nz // 2, C_ROWS, LANES), f32),
            pltpu.VMEM((2 * D, LANES), f32),
            dma((5,)),
            dma((3,)),
            dma((2, NEAR)),
            dma((2, nz)),
            dma((2, NX)),
            dma((2,)),
            dma((2, NY)),
            dma((TILES,)),
            dma((per, nz)),
            dma((per, nz)),
            dma((TILES,)),
            dma((2, CHIPS)),
            dma((2, NX)),
            dma((2, NX)),
            dma((2, CHIPS)),
            dma((2,)),
            dma((2, nz // 2)),
            dma((2,)),
            dma((2, CHIPS)),
            dma((2, NX)),
        ],
        compiler_params=pltpu.CompilerParams(
            collective_id=0, has_side_effects=True, vmem_limit_bytes=VMEM_BYTES
        ),
    )(slab_sizes, positive_ids.reshape(1, Q_DEV), queries_in, head_weight, codebook, codes.T)
    outs = [(1, Q_DEV), (HEAD_ROWS, D), (M, K * SUB)]
    loss, head_grad, book = pl.pallas_call(
        finish_kernel,
        out_shape=[jax.ShapeDtypeStruct(shape, f32) for shape in outs],
        in_specs=[left] * 3,
        out_specs=[left] * 3,
        scratch_shapes=[pltpu.VMEM(shape, f32) for shape in outs] + [dma((2, 6))],
        compiler_params=pltpu.CompilerParams(vmem_limit_bytes=VMEM_BYTES),
    )(loss, head_grad, book)
    return loss.reshape(Q_DEV), head_grad, book


def solution(mesh):
    nz = mesh.shape["corpus"] // (2 * NY)
    return jax.shard_map(
        functools.partial(step, nz),
        mesh=mesh,
        in_specs=(P("query", None), P(), P(), P("corpus", None), P("corpus"), P("query")),
        out_specs=(P("query"), P("query", None), P()),
        check_vma=False,
    )
```

```python
import functools

import jax
import jax.numpy as jnp
from jax import lax
from jax.experimental import pallas as pl
from jax.experimental.pallas import tpu as pltpu
from jax.sharding import PartitionSpec as P

D = 768
M = 96
K = 256
SUB = 8
SLOT_DEV = 384
Q_DEV = 128
LANES = 128
NX = 4
NY = 4
CHIPS = NX * NY
HALF = D // 2
G_ROWS = HALF // NY
C_ROWS = HALF // CHIPS
C_SUBS = C_ROWS // SUB
HEAD_ROWS = D // NX
TILES = 6
G_TILE = G_ROWS // TILES
NEAR = 2 * NY
MESH = pl.DeviceIdType.MESH
NT = (((1,), (1,)), ((), ()))
VMEM_BYTES = 48 * 1024 * 1024


def loop(start, count, act):
    def body(step, carry):
        act(step)
        return carry

    lax.fori_loop(start, count, body, 0)


def spread(a):
    return 2 - a + 3 * (a // 2) - 2 * (a // 3)


def step_kernel(
    nz,
    length_ref, ids_hbm, qin_hbm, weight_hbm, codebook_hbm, codes_hbm,
    loss, head, out,
    ids, qin, weight, codebook, codes, table, pt, qt, qint, pgt, stats, near, far, mid, book,
    pu, sides, mass, fixed, scaled,
    q_all, grad, g_core, g_send, g_block, g_sum, g_z, g_red, g_fin,
    c_core, c_send, c_block, c_half, c_many, c_fin,
    in_sems, near_sems, far_sems,
    q_sems, gc_sems, gy_sems, gz_send, gz_recv, gr_send, gr_recv, gf_sems, gs_sems,
    cc_sems, cy_sems, cz_sems, cf_sems, cs_sems,
):
    me = lax.axis_index("corpus")
    x, y, z, core = lax.axis_index("query"), me // (2 * nz), lax.rem(me // 2, nz), lax.rem(me, 2)
    other = 1 - core
    group = y * 2 + core

    def device(to_x, to_y, to_z, to_core):
        return {"corpus": (to_y * nz + to_z) * 2 + to_core, "query": to_x}

    sibling = device(x, y, z, other)

    def around(o):
        return device(x, o // 2, z, lax.rem(o, 2))

    def along(o):
        return device(x, y, o, core)

    def hop(e, ring=nz):
        return ring // 2 + ((e + 1) // 2) * (1 - 2 * lax.rem(e, 2))

    def chip_at(s, sign):
        to_x = lax.rem(x + 4 + sign * spread(s // 4), NX)
        to_y = lax.rem(y + 4 + sign * spread(lax.rem(s, 4)), NY)
        return to_x, to_y

    def place_at(s, sign):
        to_x, to_y = chip_at(s, sign)
        return to_x * NY + to_y

    def chip(s, sign=1):
        to_x, to_y = chip_at(s, sign)
        return device(to_x, to_y, z, core)

    odd, pair, pairs = lax.rem(z, 2), z // 2, nz // 2

    def chip_beside(s):
        to_x, to_y = chip_at(s, 1)
        return device(to_x, to_y, z + 1 - 2 * odd, core)

    def half_at(which):
        return pl.ds(pl.multiple_of(which * C_ROWS, 8), C_ROWS)

    def y_at(d):
        return lax.rem(y + d, NY)

    def copy(src, dst, send, recv, to):
        return pltpu.make_async_remote_copy(
            src_ref=src, dst_ref=dst, send_sem=send, recv_sem=recv, device_id=to, device_id_type=MESH
        )

    barrier = pltpu.get_barrier_semaphore()

    def greet(to):
        pl.semaphore_signal(barrier, 1, device_id=to, device_id_type=MESH)

    loop(0, nz - 1, lambda e: greet(along(lax.rem(z + hop(e), nz))))
    loads = [
        pltpu.make_async_copy(src, dst, in_sems.at[i])
        for i, (src, dst) in enumerate(
            [(codebook_hbm, codebook), (codes_hbm, codes), (qin_hbm, qin), (weight_hbm, weight), (ids_hbm, ids)]
        )
    ]
    for load in loads:
        load.start()
    loop(1, NEAR, lambda d: greet(around(lax.rem(group + d, NEAR))))
    loop(0, 12, lambda s: greet(chip(s)))
    loop(0, CHIPS - 1, lambda s: greet(chip_beside(s)))

    wide = K * SUB // 2
    down = lax.broadcasted_iota(jnp.int32, (wide, wide), 0)
    across = lax.broadcasted_iota(jnp.int32, (wide, wide), 1)
    pick = down == (across % LANES) * SUB + across // LANES
    pick = jnp.where(pick, jnp.float32(1), jnp.float32(0)).astype(jnp.bfloat16)
    loads[0].wait()
    for part in range(2):
        words = jnp.dot(
            codebook[:, part * wide : (part + 1) * wide], pick, preferred_element_type=jnp.float32
        )
        for j in range(SUB):
            table[pl.ds(part * D + j, M, stride=SUB), :] = words[:, j * LANES : (j + 1) * LANES]
    loads[1].wait()

    def rebuild(pair, carry):
        halves = []
        for part in range(2):
            m = pair * 2 + part
            lower = table[pl.ds(pl.multiple_of(m * SUB, SUB), SUB), :]
            upper = table[pl.ds(pl.multiple_of(D + m * SUB, SUB), SUB), :]
            row = codes[pl.ds(m, 1), :]
            parts = []
            for tile in range(SLOT_DEV // LANES):
                index = jnp.broadcast_to(row[:, tile * LANES : (tile + 1) * LANES], (SUB, LANES))
                low = index & (LANES - 1)
                first = jnp.take_along_axis(lower, low, axis=1, mode="promise_in_bounds")
                second = jnp.take_along_axis(upper, low, axis=1, mode="promise_in_bounds")
                parts.append(jnp.where(index >= LANES, second, first))
            halves.append(jnp.concatenate(parts, axis=1))
        rows = jnp.concatenate(halves, axis=0).astype(jnp.bfloat16)
        pt[pl.ds(pl.multiple_of(pair * 2 * SUB, 2 * SUB), 2 * SUB), :] = rows
        return carry

    lax.fori_loop(0, M // 2, rebuild, 0, unroll=4)

    loads[2].wait()
    loads[3].wait()
    loads[4].wait()
    query = jnp.dot(qin[...], weight[...], preferred_element_type=jnp.float32).astype(jnp.bfloat16)
    scores = jnp.dot(query, pt[...], preferred_element_type=jnp.float32).T
    slot = lax.broadcasted_iota(jnp.int32, (SLOT_DEV, Q_DEV), 0)
    scores = jnp.where(slot < length_ref[0], scores, -jnp.inf)
    owned = slot == ids[...] - me * SLOT_DEV
    peak = jnp.max(scores, axis=0, keepdims=True)
    raised = jnp.exp(scores - peak)
    total = jnp.sum(raised, axis=0, keepdims=True)
    positive = jnp.sum(jnp.where(owned, scores, 0.0), axis=0, keepdims=True)
    pad = jnp.zeros((5, Q_DEV), jnp.float32)
    stats[...] = jnp.concatenate([peak, total, positive, pad], axis=0)
    pl.semaphore_wait(barrier, NEAR - 1 + nz - 1 + 12 + CHIPS - 1)

    def merge(slots):
        peaks, totals, positives = slots[:, 0, :], slots[:, 1, :], slots[:, 2, :]
        peak = jnp.max(peaks, axis=0, keepdims=True)
        total = jnp.sum(totals * jnp.exp(peaks - peak), axis=0, keepdims=True)
        return peak, total, jnp.sum(positives, axis=0, keepdims=True)

    def near_copy(d):
        to = around(lax.rem(group + d, NEAR))
        return copy(stats, near.at[group], near_sems.at[0, d], near_sems.at[1, d], to)

    def far_copy(e):
        to = along(lax.rem(z + hop(e), nz))
        return copy(mid, far.at[z], far_sems.at[0, e], far_sems.at[1, e], to)

    def q_copy(d):
        to = lax.rem(x + d, NX)
        rows = pl.ds(pl.multiple_of(to * HEAD_ROWS, 16), HEAD_ROWS)
        return copy(qint.at[rows], q_all.at[x], q_sems.at[0, d], q_sems.at[1, d], device(to, y, z, core))

    def onto(m):
        rows = pl.ds(pl.multiple_of(m * SUB, SUB), SUB)
        part = pgt[rows, :]
        upper = part.astype(jnp.bfloat16)
        lower = (part - upper.astype(jnp.float32)).astype(jnp.bfloat16)
        code = codes[pl.ds(m, 1), :].astype(jnp.float32).astype(jnp.bfloat16)
        onehot = jnp.where(word == code, jnp.bfloat16(1), jnp.bfloat16(0))
        left = jnp.concatenate([pu[...], upper, lower], axis=0)
        sums = lax.dot_general(left, onehot, NT, preferred_element_type=jnp.float32)
        mass[pl.ds(pl.multiple_of(m * Q_DEV, Q_DEV), Q_DEV), :] = sums[:Q_DEV].astype(jnp.bfloat16)
        fixed[rows, :] = sums[Q_DEV : Q_DEV + SUB] + sums[Q_DEV + SUB :]

    def onto_range(first, last):
        def body(m, carry):
            onto(m)
            return carry

        lax.fori_loop(first, last, body, 0, unroll=4)

    def g_core_copy():
        rows = pl.ds(other * (HALF // 16), HALF // 16)
        return copy(grad.at[rows], g_core, gc_sems.at[0], gc_sems.at[1], sibling)

    def g_y_copy(d):
        to = device(x, y_at(d), z, core)
        return copy(g_send.at[d], g_block.at[d], gy_sems.at[0, d], gy_sems.at[1, d], to)

    def g_pair(d):
        first = y_at(d) * TILES
        mine = grad[pl.ds(core * (HALF // 16) + first, TILES)].astype(jnp.float32)
        return mine + g_core[pl.ds(first, TILES)].astype(jnp.float32)

    def g_go(d):
        g_send[d] = g_pair(d).astype(jnp.bfloat16)
        g_y_copy(d).start()

    loop(1, NEAR, lambda d: near_copy(d).start())
    near[group] = stats[...]
    qt[...] = query.astype(jnp.float32).T.astype(jnp.bfloat16)
    qint[...] = qin[...].astype(jnp.float32).T.astype(jnp.bfloat16)
    pu[...] = raised.T.astype(jnp.bfloat16)
    minus = jnp.where(owned, -1.0, 0.0).astype(jnp.bfloat16)
    both = jnp.concatenate([raised.astype(jnp.bfloat16), minus], axis=1)
    sides[...] = jnp.dot(pt[...], both, preferred_element_type=jnp.float32)
    pgt[...] = lax.dot_general(qt[...], minus, NT, preferred_element_type=jnp.float32)
    word = lax.broadcasted_iota(jnp.int32, (K, SLOT_DEV), 0).astype(jnp.float32)
    word = word.astype(jnp.bfloat16)
    onto_range(0, 12)
    loop(1, NEAR, lambda d: near_copy(d).wait_recv())
    near_peak, near_total, near_positive = merge(near[...])
    mid[...] = jnp.concatenate([near_peak, near_total, near_positive, pad], axis=0)
    loop(0, nz - 1, lambda e: far_copy(e).start())
    far[z] = mid[...]

    tiles = (D // 16, 16, Q_DEV)
    soft = sides[:, :Q_DEV] * jnp.exp(peak - near_peak)
    grad[:, 0] = soft.astype(jnp.bfloat16).reshape(tiles)
    grad[:, 1] = sides[:, Q_DEV:].astype(jnp.bfloat16).reshape(tiles)
    g_core_copy().start()
    loop(1, NX, lambda d: q_copy(d).start())
    q_all[x] = qint[pl.ds(pl.multiple_of(x * HEAD_ROWS, 16), HEAD_ROWS), :]
    onto_range(12, 24)
    g_core_copy().wait_recv()
    loop(1, NY, g_go)
    onto_range(24, 72)

    def g_part(t):
        return (pl.ds(t * G_TILE, G_TILE), slice(None))

    def g_owner(t):
        return (t * nz) // TILES

    def g_place(t):
        return sum(1 for s in range(t) if g_owner(s) == g_owner(t))

    def z_copy(t):
        p = g_place(t)
        return copy(g_sum.at[t], g_z.at[p, z], gz_send.at[t], gz_recv.at[p, z], along(g_owner(t)))

    def z_heard(t, o):
        p = g_place(t)
        return copy(g_z.at[p, o], g_z.at[p, o], gz_send.at[t], gz_recv.at[p, o], along(o))

    g_final = g_fin.at[x, core, y]

    def back_copy(t, e):
        to = along(lax.rem(z + hop(e), nz))
        return copy(g_red.at[g_place(t)], g_final.at[g_part(t)], gr_send.at[g_place(t), e], gr_recv.at[t], to)

    loop(1, NY, lambda d: g_y_copy(d).wait_recv())
    g_total = g_pair(0)
    for d in range(1, NY):
        g_total = g_total + g_block[d].astype(jnp.float32)
    g_sum[...] = g_total.astype(jnp.bfloat16)
    for t in range(TILES):

        @pl.when(z == g_owner(t))
        def _(t=t):
            g_z[g_place(t), z] = g_sum[t]

        @pl.when(z != g_owner(t))
        def _(t=t):
            z_copy(t).start()

    onto_range(72, M)
    loop(0, nz - 1, lambda e: far_copy(e).wait_recv())
    last_peak, total, positive = merge(far[...])
    log_total = last_peak + jnp.log(total)
    loss[...] = log_total - positive
    scaled[...] = qt[...].astype(jnp.float32) * jnp.exp(peak - log_total)

    def split(m):
        part = scaled[pl.ds(pl.multiple_of(m * SUB, SUB), SUB), :]
        upper = part.astype(jnp.bfloat16)
        lower = (part - upper.astype(jnp.float32)).astype(jnp.bfloat16)
        return jnp.concatenate([upper, lower], axis=0)

    def x_at(a, sign=1):
        return lax.rem(x + 4 + sign * spread(a), NX)

    def c_compute(side, a):
        for i in range(0, NY * C_SUBS, 2):
            m = side * (M // 2) + x_at(a) * (NY * C_SUBS) + i
            nil = jnp.zeros((2 * SUB, Q_DEV), jnp.bfloat16)
            first = jnp.concatenate([split(m), nil], axis=1)
            second = jnp.concatenate([nil, split(m + 1)], axis=1)
            both_of = mass[pl.ds(pl.multiple_of(m * Q_DEV, Q_DEV), 2 * Q_DEV), :]
            sums = jnp.dot(
                jnp.concatenate([first, second], axis=0), both_of, preferred_element_type=jnp.float32
            )
            rows = pl.ds(pl.multiple_of(m * SUB, SUB), 2 * SUB)
            sums = [sums[k * SUB : (k + 1) * SUB] for k in range(4)]
            book[rows, :] = jnp.concatenate([sums[0] + sums[1], sums[2] + sums[3]], axis=0) + fixed[rows, :]

    def c_core_copy(a):
        rows = pl.ds(pl.multiple_of(other * HALF + x_at(a) * NY * C_ROWS, 8), NY * C_ROWS)
        return copy(book.at[rows], c_core.at[a], cc_sems.at[0, a], cc_sems.at[1, a], sibling)

    def c_chip_copy(s):
        return copy(
            c_send.at[s, half_at(odd)], c_block.at[s], cy_sems.at[0, s], cy_sems.at[1, s], chip(s)
        )

    def c_beside_copy(s):
        k = CHIPS + s
        return copy(
            c_send.at[s, half_at(1 - odd)], c_block.at[k], cy_sems.at[0, k], cy_sems.at[1, k], chip_beside(s)
        )

    def c_add(s):
        to_x, to_y = chip_at(s, 1)
        rows = pl.ds(pl.multiple_of(core * HALF + (to_x * NY + to_y) * C_ROWS, 8), C_ROWS)
        there = pl.ds(pl.multiple_of(to_y * C_ROWS, 8), C_ROWS)
        both = book[rows, :] + c_core[s // NY, there, :]
        for i in range(C_SUBS):
            for part in range(2):
                tile = both[i * SUB : (i + 1) * SUB, part * LANES : (part + 1) * LANES]
                c_send[s, pl.ds((2 * i + part) * SUB, SUB), :] = tile

    def c_go(s):
        c_add(s)
        c_beside_copy(s).start()
        c_chip_copy(s).start()

    def c_near(a):
        c_compute(other, a)
        c_core_copy(a).start()

    def c_away(a, count):
        c_compute(core, a)
        c_core_copy(a).wait_recv()
        loop(a * NY, a * NY + count, c_go)

    loop(0, NX, c_near)
    loop(0, NX - 1, lambda a: c_away(a, NY))
    c_away(NX - 1, NY - 1)
    c_add(CHIPS - 1)
    c_beside_copy(CHIPS - 1).start()

    for t in range(TILES):

        @pl.when(z == g_owner(t))
        def _(t=t):
            loop(0, nz - 1, lambda e: z_heard(t, lax.rem(z + hop(e), nz)).wait_recv())
            weights = jnp.exp(far[...][:, 0, :] - log_total)
            whole = jnp.zeros((16, Q_DEV), jnp.float32)
            for o in range(nz):
                whole = whole + g_z[g_place(t), o, 0].astype(jnp.float32) * weights[o : o + 1, :]
                whole = whole + g_z[g_place(t), o, 1].astype(jnp.float32)
            g_red[g_place(t)] = whole.astype(jnp.bfloat16)
            loop(0, nz - 1, lambda e: back_copy(t, e).start())
            g_final[g_part(t)] = whole.astype(jnp.bfloat16)

    def interleave(tile):
        down = lax.broadcasted_iota(jnp.int32, (SUB, LANES), 0)
        across = lax.broadcasted_iota(jnp.int32, (SUB, LANES), 1)
        index = down * (LANES // SUB) + across // SUB
        mixed = jnp.zeros((SUB, LANES), jnp.float32)
        for j in range(SUB):
            row = jnp.broadcast_to(tile[j : j + 1, :], (SUB, LANES))
            row = jnp.take_along_axis(row, index, axis=1, mode="promise_in_bounds")
            mixed = jnp.where(across % SUB == j, row, mixed)
        return mixed

    loop(0, CHIPS - 1, lambda s: c_chip_copy(s).wait_recv())
    loop(0, CHIPS, lambda s: c_beside_copy(s).wait_recv())
    c_total = c_send[CHIPS - 1, half_at(odd), :]
    for s in range(2 * CHIPS):
        if s != CHIPS - 1:
            c_total = c_total + c_block[s]

    def c_many_copy(e):
        to = along(lax.rem(pair + hop(e, pairs), pairs) * 2 + odd)
        return copy(c_half, c_many.at[pair], cz_sems.at[0, e], cz_sems.at[1, e], to)

    c_half[...] = c_total
    c_many[pair] = c_total
    loop(0, pairs - 1, lambda e: c_many_copy(e).start())

    def c_final_at(side, place):
        return c_fin.at[pl.ds(pl.multiple_of((side * CHIPS + place) * 2 * C_ROWS, 8), 2 * C_ROWS)]

    c_final = c_final_at(core, x * NY + y)
    def g_at(side, s):
        from_x, from_y = chip_at(s, -1)
        return g_fin.at[from_x, side, from_y]

    def g_out(s):
        return copy(g_final, g_final, gf_sems.at[0, s], gf_sems.at[1, s], chip(s))

    def g_in(s):
        return copy(g_at(core, s), g_at(core, s), gf_sems.at[0, s], gf_sems.at[1, s], chip(s))

    def g_row(side, a):
        return g_fin.at[x_at(a, -1), side]

    def g_share(a):
        return copy(g_row(core, a), g_row(core, a), gs_sems.at[0, a], gs_sems.at[1, a], sibling)

    def g_shared(a):
        return copy(g_row(other, a), g_row(other, a), gs_sems.at[0, a], gs_sems.at[1, a], sibling)

    def c_out(s):
        mine = c_final.at[half_at(odd)]
        return copy(mine, mine, cf_sems.at[0, s], cf_sems.at[1, s], chip(s))

    def c_out_beside(s):
        mine = c_final.at[half_at(odd)]
        return copy(mine, mine, cf_sems.at[0, CHIPS + s], cf_sems.at[1, CHIPS + s], chip_beside(s))

    def c_at(side, s):
        return c_final_at(side, place_at(s, -1))

    def c_in(s):
        came = c_at(core, s).at[half_at(odd)]
        return copy(came, came, cf_sems.at[0, s], cf_sems.at[1, s], chip(s))

    def c_in_beside(s):
        came = c_at(core, s).at[half_at(1 - odd)]
        return copy(came, came, cf_sems.at[0, CHIPS + s], cf_sems.at[1, CHIPS + s], chip(s))

    def c_row(side, a):
        first = (side * CHIPS + x_at(a, -1) * NY) * 2 * C_ROWS
        return c_fin.at[pl.ds(pl.multiple_of(first, 8), NY * 2 * C_ROWS)]

    def c_share(a):
        return copy(c_row(core, a), c_row(core, a), cs_sems.at[0, a], cs_sems.at[1, a], sibling)

    def c_shared(a):
        return copy(c_row(other, a), c_row(other, a), cs_sems.at[0, a], cs_sems.at[1, a], sibling)

    for t in range(TILES):

        @pl.when(z != g_owner(t))
        def _(t=t):
            back_copy(t, 0).wait_recv()

    loop(0, CHIPS - 1, lambda s: g_out(s).start())
    loop(0, pairs - 1, lambda e: c_many_copy(e).wait_recv())
    c_total = c_many[0]
    for o in range(1, pairs):
        c_total = c_total + c_many[o]
    first = pl.multiple_of(odd * C_ROWS, 8)
    for i in range(C_SUBS):
        c_final[pl.ds(pl.multiple_of(first + i * SUB, 8), SUB), :] = interleave(
            c_total[i * SUB : (i + 1) * SUB]
        )


    def c_spread(s):
        c_out_beside(s).start()
        c_out(s).start()

    loop(0, CHIPS - 1, c_spread)
    c_out_beside(CHIPS - 1).start()

    def pass_on(came, share):
        def act(a):
            loop(a * NY, lax.min(a * NY + NY, CHIPS - 1), lambda s: came(s).wait_recv())
            share(a).start()

        loop(0, NX, act)

    pass_on(g_in, g_share)
    loop(1, NX, lambda d: q_copy(d).wait_recv())
    loop(0, NX, lambda a: g_shared(a).wait_recv())
    total = jnp.zeros((HEAD_ROWS, D), jnp.float32)
    for o in range(NX):
        total = total + lax.dot_general(
            q_all[o], g_fin[o].reshape(D, Q_DEV), NT, preferred_element_type=jnp.float32
        )
    head[...] = total

    def c_pass(a):
        loop(a * NY, lax.min(a * NY + NY, CHIPS - 1), lambda s: c_in(s).wait_recv())
        loop(a * NY, a * NY + NY, lambda s: c_in_beside(s).wait_recv())
        c_share(a).start()

    loop(0, NX, c_pass)
    loop(0, NX, lambda a: c_shared(a).wait_recv())
    for u in range(2 * SUB):
        out[:, u * LANES : (u + 1) * LANES] = c_fin[pl.ds(u, M, stride=2 * SUB), :]

    loop(1, NEAR, lambda d: near_copy(d).wait_send())
    loop(0, nz - 1, lambda e: far_copy(e).wait_send())
    loop(1, NX, lambda d: q_copy(d).wait_send())
    g_core_copy().wait_send()
    loop(0, NX, lambda a: c_core_copy(a).wait_send())
    loop(1, NY, lambda d: g_y_copy(d).wait_send())
    loop(0, CHIPS - 1, lambda s: c_chip_copy(s).wait_send())
    for t in range(TILES):

        @pl.when(z == g_owner(t))
        def _(t=t):
            loop(0, nz - 1, lambda e: back_copy(t, e).wait_send())

        @pl.when(z != g_owner(t))
        def _(t=t):
            z_copy(t).wait_send()

    loop(0, CHIPS, lambda s: c_beside_copy(s).wait_send())
    loop(0, pairs - 1, lambda e: c_many_copy(e).wait_send())
    loop(0, CHIPS - 1, lambda s: g_out(s).wait_send())
    loop(0, NX, lambda a: g_share(a).wait_send())
    loop(0, CHIPS - 1, lambda s: c_out(s).wait_send())
    loop(0, CHIPS, lambda s: c_out_beside(s).wait_send())
    loop(0, NX, lambda a: c_share(a).wait_send())


def finish_kernel(loss_in, head_in, book_in, loss_out, head_out, book_out, sems):
    moves = [(loss_in, loss_out)]
    for i in range(3):
        rows = pl.ds(i * (M // 3), M // 3)
        moves.append((book_in.at[rows], book_out.at[rows]))
    for i in range(2):
        rows = pl.ds(i * (HEAD_ROWS // 2), HEAD_ROWS // 2)
        moves.append((head_in.at[rows], head_out.at[rows]))
    copies = [pltpu.make_async_copy(src, dst, sems.at[i]) for i, (src, dst) in enumerate(moves)]
    for each in copies:
        each.start()
    for each in copies:
        each.wait()


def step(nz, queries_in, head_weight, codebook, codes, slab_sizes, positive_ids):
    left = pl.BlockSpec(memory_space=pltpu.HBM)
    whole = pl.BlockSpec(memory_space=pltpu.VMEM)
    dma = pltpu.SemaphoreType.DMA
    f32, bf16 = jnp.float32, jnp.bfloat16
    per = -(-TILES // nz)
    outs = [(1, Q_DEV), (HEAD_ROWS, D), (M, K * SUB)]
    ins = [positive_ids.reshape(1, Q_DEV), queries_in, head_weight, codebook, codes.T]
    ins = [pltpu.with_memory_space_constraint(each, pltpu.HBM) for each in ins]
    loss, head_grad, book = pl.pallas_call(
        functools.partial(step_kernel, nz),
        out_shape=[pltpu.VMEM(shape, f32) for shape in outs],
        in_specs=[pl.BlockSpec(memory_space=pltpu.SMEM)] + [left] * 5,
        out_specs=[whole] * 3,
        scratch_shapes=[
            pltpu.VMEM((1, Q_DEV), jnp.int32),
            pltpu.VMEM((Q_DEV, D), bf16),
            pltpu.VMEM((D, D), bf16),
            pltpu.VMEM((M, K * SUB), bf16),
            pltpu.VMEM((M, SLOT_DEV), jnp.int32),
            pltpu.VMEM((2 * D, LANES), f32),
            pltpu.VMEM((D, SLOT_DEV), bf16),
            pltpu.VMEM((D, Q_DEV), bf16),
            pltpu.VMEM((D, Q_DEV), bf16),
            pltpu.VMEM((D, SLOT_DEV), f32),
            pltpu.VMEM((8, Q_DEV), f32),
            pltpu.VMEM((NEAR, 8, Q_DEV), f32),
            pltpu.VMEM((nz, 8, Q_DEV), f32),
            pltpu.VMEM((8, Q_DEV), f32),
            pltpu.VMEM((D, K), f32),
            pltpu.VMEM((Q_DEV, SLOT_DEV), bf16),
            pltpu.VMEM((D, 2 * Q_DEV), f32),
            pltpu.VMEM((M * Q_DEV, K), bf16),
            pltpu.VMEM((D, K), f32),
            pltpu.VMEM((D, Q_DEV), f32),
            pltpu.VMEM((NX, HEAD_ROWS, Q_DEV), bf16),
            pltpu.VMEM((D // 16, 2, 16, Q_DEV), bf16),
            pltpu.VMEM((HALF // 16, 2, 16, Q_DEV), bf16),
            pltpu.VMEM((NY, TILES, 2, 16, Q_DEV), bf16),
            pltpu.VMEM((NY, TILES, 2, 16, Q_DEV), bf16),
            pltpu.VMEM((TILES, 2, 16, Q_DEV), bf16),
            pltpu.VMEM((per, nz, 2, 16, Q_DEV), bf16),
            pltpu.VMEM((per, 16, Q_DEV), bf16),
            pltpu.VMEM((NX, 2, NY, G_ROWS, Q_DEV), bf16),
            pltpu.VMEM((NX, NY * C_ROWS, K), f32),
            pltpu.VMEM((CHIPS, 2 * C_ROWS, LANES), f32),
            pltpu.VMEM((2 * CHIPS, C_ROWS, LANES), f32),
            pltpu.VMEM((C_ROWS, LANES), f32),
            pltpu.VMEM((nz // 2, C_ROWS, LANES), f32),
            pltpu.VMEM((2 * D, LANES), f32),
            dma((5,)),
            dma((2, NEAR)),
            dma((2, nz)),
            dma((2, NX)),
            dma((2,)),
            dma((2, NY)),
            dma((TILES,)),
            dma((per, nz)),
            dma((per, nz)),
            dma((TILES,)),
            dma((2, CHIPS)),
            dma((2, NX)),
            dma((2, NX)),
            dma((2, 2 * CHIPS)),
            dma((2, nz // 2)),
            dma((2, 2 * CHIPS)),
            dma((2, NX)),
        ],
        compiler_params=pltpu.CompilerParams(
            collective_id=0, has_side_effects=True, vmem_limit_bytes=VMEM_BYTES
        ),
    )(slab_sizes, *ins)
    loss, head_grad, book = pl.pallas_call(
        finish_kernel,
        out_shape=[jax.ShapeDtypeStruct(shape, f32) for shape in outs],
        in_specs=[whole] * 3,
        out_specs=[left] * 3,
        scratch_shapes=[dma((6,))],
        compiler_params=pltpu.CompilerParams(vmem_limit_bytes=VMEM_BYTES),
    )(loss, head_grad, book)
    return loss.reshape(Q_DEV), head_grad, book


def solution(mesh):
    nz = mesh.shape["corpus"] // (2 * NY)
    return jax.shard_map(
        functools.partial(step, nz),
        mesh=mesh,
        in_specs=(P("query", None), P(), P(), P("corpus", None), P("corpus"), P("query")),
        out_specs=(P("query"), P("query", None), P()),
        check_vma=False,
    )
```

```python
import functools

import jax
import jax.numpy as jnp
from jax import lax
from jax.experimental import pallas as pl
from jax.experimental.pallas import tpu as pltpu
from jax.sharding import PartitionSpec as P

D = 768
M = 96
K = 256
SUB = 8
SLOT_DEV = 384
Q_DEV = 128
LANES = 128
NX = 4
NY = 4
CHIPS = NX * NY
HALF = D // 2
G_ROWS = HALF // NY
C_ROWS = HALF // CHIPS
C_SUBS = C_ROWS // SUB
HEAD_ROWS = D // NX
TILES = 6
G_TILE = G_ROWS // TILES
NEAR = 2 * NY
MESH = pl.DeviceIdType.MESH
NT = (((1,), (1,)), ((), ()))
VMEM_BYTES = 48 * 1024 * 1024


def loop(start, count, act):
    if isinstance(start, int) and isinstance(count, int):
        for step in range(start, count):
            act(step)
        return
    def body(step, carry):
        act(step)
        return carry

    lax.fori_loop(start, count, body, 0)


def spread(a):
    return 2 - a + 3 * (a // 2) - 2 * (a // 3)


def step_kernel(
    nz,
    length_ref, ids_hbm, qin_hbm, weight_hbm, codebook_hbm, codes_hbm,
    loss, head, out,
    ids, qin, weight, codebook, codes, table, pt, qt, qint, pgt, stats, near, far, mid, book,
    pu, sides, mass, fixed, scaled,
    q_all, grad, g_core, g_send, g_block, g_sum, g_z, g_red, g_fin,
    c_core, c_send, c_block, c_half, c_many, c_fin,
    in_sems, near_sems, far_sems,
    q_sems, gc_sems, gy_sems, gz_send, gz_recv, gr_send, gr_recv, gf_sems, gs_sems,
    cc_sems, cy_sems, cz_sems, cf_sems, cs_sems,
):
    me = lax.axis_index("corpus")
    x, y, z, core = lax.axis_index("query"), me // (2 * nz), lax.rem(me // 2, nz), lax.rem(me, 2)
    other = 1 - core
    group = y * 2 + core

    def device(to_x, to_y, to_z, to_core):
        return {"corpus": (to_y * nz + to_z) * 2 + to_core, "query": to_x}

    sibling = device(x, y, z, other)

    def around(o):
        return device(x, o // 2, z, lax.rem(o, 2))

    def along(o):
        return device(x, y, o, core)

    def hop(e, ring=nz):
        return ring // 2 + ((e + 1) // 2) * (1 - 2 * (e % 2))

    def chip_at(s, sign):
        to_x = lax.rem(x + 4 + sign * spread(s // 4), NX)
        to_y = lax.rem(y + 4 + sign * spread(s % 4), NY)
        return to_x, to_y

    def place_at(s, sign):
        to_x, to_y = chip_at(s, sign)
        return to_x * NY + to_y

    def chip(s, sign=1):
        to_x, to_y = chip_at(s, sign)
        return device(to_x, to_y, z, core)

    odd, pair, pairs = lax.rem(z, 2), z // 2, nz // 2

    def chip_beside(s):
        to_x, to_y = chip_at(s, 1)
        return device(to_x, to_y, z + 1 - 2 * odd, core)

    def half_at(which):
        return pl.ds(pl.multiple_of(which * C_ROWS, 8), C_ROWS)

    def y_at(d):
        return lax.rem(y + d, NY)

    def copy(src, dst, send, recv, to):
        return pltpu.make_async_remote_copy(
            src_ref=src, dst_ref=dst, send_sem=send, recv_sem=recv, device_id=to, device_id_type=MESH
        )

    barrier = pltpu.get_barrier_semaphore()

    def greet(to):
        pl.semaphore_signal(barrier, 1, device_id=to, device_id_type=MESH)

    loop(0, nz - 1, lambda e: greet(along(lax.rem(z + hop(e), nz))))
    loads = [
        pltpu.make_async_copy(src, dst, in_sems.at[i])
        for i, (src, dst) in enumerate(
            [(codebook_hbm, codebook), (codes_hbm, codes), (qin_hbm, qin), (weight_hbm, weight), (ids_hbm, ids)]
        )
    ]
    for load in loads:
        load.start()
    loop(1, NEAR, lambda d: greet(around(lax.rem(group + d, NEAR))))
    loop(0, 12, lambda s: greet(chip(s)))
    loop(0, CHIPS - 1, lambda s: greet(chip_beside(s)))

    wide = K * SUB // 2
    down = lax.broadcasted_iota(jnp.int32, (wide, wide), 0)
    across = lax.broadcasted_iota(jnp.int32, (wide, wide), 1)
    pick = down == (across % LANES) * SUB + across // LANES
    pick = jnp.where(pick, jnp.float32(1), jnp.float32(0)).astype(jnp.bfloat16)
    loads[0].wait()
    for part in range(2):
        words = jnp.dot(
            codebook[:, part * wide : (part + 1) * wide], pick, preferred_element_type=jnp.float32
        )
        for j in range(SUB):
            table[pl.ds(part * D + j, M, stride=SUB), :] = words[:, j * LANES : (j + 1) * LANES]
    loads[1].wait()

    def rebuild(pair, carry):
        halves = []
        for part in range(2):
            m = pair * 2 + part
            lower = table[pl.ds(pl.multiple_of(m * SUB, SUB), SUB), :]
            upper = table[pl.ds(pl.multiple_of(D + m * SUB, SUB), SUB), :]
            row = codes[pl.ds(m, 1), :]
            parts = []
            for tile in range(SLOT_DEV // LANES):
                index = jnp.broadcast_to(row[:, tile * LANES : (tile + 1) * LANES], (SUB, LANES))
                low = index & (LANES - 1)
                first = jnp.take_along_axis(lower, low, axis=1, mode="promise_in_bounds")
                second = jnp.take_along_axis(upper, low, axis=1, mode="promise_in_bounds")
                parts.append(jnp.where(index >= LANES, second, first))
            halves.append(jnp.concatenate(parts, axis=1))
        rows = jnp.concatenate(halves, axis=0).astype(jnp.bfloat16)
        pt[pl.ds(pl.multiple_of(pair * 2 * SUB, 2 * SUB), 2 * SUB), :] = rows
        return carry

    lax.fori_loop(0, M // 2, rebuild, 0, unroll=4)

    loads[2].wait()
    loads[3].wait()
    loads[4].wait()
    query = jnp.dot(qin[...], weight[...], preferred_element_type=jnp.float32).astype(jnp.bfloat16)
    scores = jnp.dot(query, pt[...], preferred_element_type=jnp.float32).T
    slot = lax.broadcasted_iota(jnp.int32, (SLOT_DEV, Q_DEV), 0)
    scores = jnp.where(slot < length_ref[0], scores, -jnp.inf)
    owned = slot == ids[...] - me * SLOT_DEV
    peak = jnp.max(scores, axis=0, keepdims=True)
    raised = jnp.exp(scores - peak)
    total = jnp.sum(raised, axis=0, keepdims=True)
    positive = jnp.sum(jnp.where(owned, scores, 0.0), axis=0, keepdims=True)
    pad = jnp.zeros((5, Q_DEV), jnp.float32)
    stats[...] = jnp.concatenate([peak, total, positive, pad], axis=0)
    pl.semaphore_wait(barrier, NEAR - 1 + nz - 1 + 12 + CHIPS - 1)

    def merge(slots):
        peaks, totals, positives = slots[:, 0, :], slots[:, 1, :], slots[:, 2, :]
        peak = jnp.max(peaks, axis=0, keepdims=True)
        total = jnp.sum(totals * jnp.exp(peaks - peak), axis=0, keepdims=True)
        return peak, total, jnp.sum(positives, axis=0, keepdims=True)

    def near_copy(d):
        to = around(lax.rem(group + d, NEAR))
        return copy(stats, near.at[group], near_sems.at[0, d], near_sems.at[1, d], to)

    def far_copy(e):
        to = along(lax.rem(z + hop(e), nz))
        return copy(mid, far.at[z], far_sems.at[0, e], far_sems.at[1, e], to)

    def q_copy(d):
        to = lax.rem(x + d, NX)
        rows = pl.ds(pl.multiple_of(to * HEAD_ROWS, 16), HEAD_ROWS)
        return copy(qint.at[rows], q_all.at[x], q_sems.at[0, d], q_sems.at[1, d], device(to, y, z, core))

    def onto(m):
        rows = pl.ds(pl.multiple_of(m * SUB, SUB), SUB)
        part = pgt[rows, :]
        upper = part.astype(jnp.bfloat16)
        lower = (part - upper.astype(jnp.float32)).astype(jnp.bfloat16)
        code = codes[pl.ds(m, 1), :].astype(jnp.float32).astype(jnp.bfloat16)
        onehot = jnp.where(word == code, jnp.bfloat16(1), jnp.bfloat16(0))
        left = jnp.concatenate([pu[...], upper, lower], axis=0)
        sums = lax.dot_general(left, onehot, NT, preferred_element_type=jnp.float32)
        mass[pl.ds(pl.multiple_of(m * Q_DEV, Q_DEV), Q_DEV), :] = sums[:Q_DEV].astype(jnp.bfloat16)
        fixed[rows, :] = sums[Q_DEV : Q_DEV + SUB] + sums[Q_DEV + SUB :]

    def onto_range(first, last):
        def body(m, carry):
            onto(m)
            return carry

        lax.fori_loop(first, last, body, 0, unroll=4)

    def g_core_copy():
        rows = pl.ds(other * (HALF // 16), HALF // 16)
        return copy(grad.at[rows], g_core, gc_sems.at[0], gc_sems.at[1], sibling)

    def g_y_copy(d):
        to = device(x, y_at(d), z, core)
        return copy(g_send.at[d], g_block.at[d], gy_sems.at[0, d], gy_sems.at[1, d], to)

    def g_pair(d):
        first = y_at(d) * TILES
        mine = grad[pl.ds(core * (HALF // 16) + first, TILES)].astype(jnp.float32)
        return mine + g_core[pl.ds(first, TILES)].astype(jnp.float32)

    def g_go(d):
        g_send[d] = g_pair(d).astype(jnp.bfloat16)
        g_y_copy(d).start()

    loop(1, NEAR, lambda d: near_copy(d).start())
    near[group] = stats[...]
    qt[...] = query.astype(jnp.float32).T.astype(jnp.bfloat16)
    qint[...] = qin[...].astype(jnp.float32).T.astype(jnp.bfloat16)
    pu[...] = raised.T.astype(jnp.bfloat16)
    minus = jnp.where(owned, -1.0, 0.0).astype(jnp.bfloat16)
    both = jnp.concatenate([raised.astype(jnp.bfloat16), minus], axis=1)
    sides[...] = jnp.dot(pt[...], both, preferred_element_type=jnp.float32)
    pgt[...] = lax.dot_general(qt[...], minus, NT, preferred_element_type=jnp.float32)
    word = lax.broadcasted_iota(jnp.int32, (K, SLOT_DEV), 0).astype(jnp.float32)
    word = word.astype(jnp.bfloat16)
    onto_range(0, 20)
    loop(1, NEAR, lambda d: near_copy(d).wait_recv())
    near_peak, near_total, near_positive = merge(near[...])
    mid[...] = jnp.concatenate([near_peak, near_total, near_positive, pad], axis=0)
    loop(0, nz - 1, lambda e: far_copy(e).start())
    far[z] = mid[...]

    tiles = (D // 16, 16, Q_DEV)
    soft = sides[:, :Q_DEV] * jnp.exp(peak - near_peak)
    grad[:, 0] = soft.astype(jnp.bfloat16).reshape(tiles)
    grad[:, 1] = sides[:, Q_DEV:].astype(jnp.bfloat16).reshape(tiles)
    g_core_copy().start()
    loop(1, NX, lambda d: q_copy(d).start())
    q_all[x] = qint[pl.ds(pl.multiple_of(x * HEAD_ROWS, 16), HEAD_ROWS), :]
    onto_range(20, 28)
    g_core_copy().wait_recv()
    loop(1, NY, g_go)
    onto_range(28, 72)

    def g_part(t):
        return (pl.ds(t * G_TILE, G_TILE), slice(None))

    def g_owner(t):
        return (t * nz) // TILES

    def g_place(t):
        return sum(1 for s in range(t) if g_owner(s) == g_owner(t))

    def z_copy(t):
        p = g_place(t)
        return copy(g_sum.at[t], g_z.at[p, z], gz_send.at[t], gz_recv.at[p, z], along(g_owner(t)))

    def z_heard(t, o):
        p = g_place(t)
        return copy(g_z.at[p, o], g_z.at[p, o], gz_send.at[t], gz_recv.at[p, o], along(o))

    g_final = g_fin.at[x, core, y]

    def back_copy(t, e):
        to = along(lax.rem(z + hop(e), nz))
        return copy(g_red.at[g_place(t)], g_final.at[g_part(t)], gr_send.at[g_place(t), e], gr_recv.at[t], to)

    loop(1, NY, lambda d: g_y_copy(d).wait_recv())
    g_total = g_pair(0)
    for d in range(1, NY):
        g_total = g_total + g_block[d].astype(jnp.float32)
    g_sum[...] = g_total.astype(jnp.bfloat16)
    for t in range(TILES):

        @pl.when(z == g_owner(t))
        def _(t=t):
            g_z[g_place(t), z] = g_sum[t]

        @pl.when(z != g_owner(t))
        def _(t=t):
            z_copy(t).start()

    onto_range(72, M)
    loop(0, nz - 1, lambda e: far_copy(e).wait_recv())
    last_peak, total, positive = merge(far[...])
    log_total = last_peak + jnp.log(total)
    loss[...] = log_total - positive
    scaled[...] = qt[...].astype(jnp.float32) * jnp.exp(peak - log_total)

    def split(m):
        part = scaled[pl.ds(pl.multiple_of(m * SUB, SUB), SUB), :]
        upper = part.astype(jnp.bfloat16)
        lower = (part - upper.astype(jnp.float32)).astype(jnp.bfloat16)
        return jnp.concatenate([upper, lower], axis=0)

    def x_at(a, sign=1):
        return lax.rem(x + 4 + sign * spread(a), NX)

    def c_compute(side, a):
        for i in range(0, NY * C_SUBS, 2):
            m = side * (M // 2) + x_at(a) * (NY * C_SUBS) + i
            nil = jnp.zeros((2 * SUB, Q_DEV), jnp.bfloat16)
            first = jnp.concatenate([split(m), nil], axis=1)
            second = jnp.concatenate([nil, split(m + 1)], axis=1)
            both_of = mass[pl.ds(pl.multiple_of(m * Q_DEV, Q_DEV), 2 * Q_DEV), :]
            sums = jnp.dot(
                jnp.concatenate([first, second], axis=0), both_of, preferred_element_type=jnp.float32
            )
            rows = pl.ds(pl.multiple_of(m * SUB, SUB), 2 * SUB)
            sums = [sums[k * SUB : (k + 1) * SUB] for k in range(4)]
            book[rows, :] = jnp.concatenate([sums[0] + sums[1], sums[2] + sums[3]], axis=0) + fixed[rows, :]

    def c_core_copy(a):
        rows = pl.ds(pl.multiple_of(other * HALF + x_at(a) * NY * C_ROWS, 8), NY * C_ROWS)
        return copy(book.at[rows], c_core.at[a], cc_sems.at[0, a], cc_sems.at[1, a], sibling)

    def c_chip_copy(s):
        return copy(
            c_send.at[s, half_at(odd)], c_block.at[s], cy_sems.at[0, s], cy_sems.at[1, s], chip(s)
        )

    def c_beside_copy(s):
        k = CHIPS + s
        return copy(
            c_send.at[s, half_at(1 - odd)], c_block.at[k], cy_sems.at[0, k], cy_sems.at[1, k], chip_beside(s)
        )

    def c_add(s):
        to_x, to_y = chip_at(s, 1)
        rows = pl.ds(pl.multiple_of(core * HALF + (to_x * NY + to_y) * C_ROWS, 8), C_ROWS)
        there = pl.ds(pl.multiple_of(to_y * C_ROWS, 8), C_ROWS)
        both = book[rows, :] + c_core[s // NY, there, :]
        for i in range(C_SUBS):
            for part in range(2):
                tile = both[i * SUB : (i + 1) * SUB, part * LANES : (part + 1) * LANES]
                c_send[s, pl.ds((2 * i + part) * SUB, SUB), :] = tile

    def c_go(s):
        c_add(s)
        c_beside_copy(s).start()
        c_chip_copy(s).start()

    def c_near(a):
        c_compute(other, a)
        c_core_copy(a).start()

    def c_away(a, count):
        c_compute(core, a)
        c_core_copy(a).wait_recv()
        loop(a * NY, a * NY + count, c_go)

    loop(0, NX, c_near)
    loop(0, NX - 1, lambda a: c_away(a, NY))
    c_away(NX - 1, NY - 1)
    c_add(CHIPS - 1)
    c_beside_copy(CHIPS - 1).start()

    for t in range(TILES):

        @pl.when(z == g_owner(t))
        def _(t=t):
            loop(0, nz - 1, lambda e: z_heard(t, lax.rem(z + hop(e), nz)).wait_recv())
            weights = jnp.exp(far[...][:, 0, :] - log_total)
            whole = jnp.zeros((16, Q_DEV), jnp.float32)
            for o in range(nz):
                whole = whole + g_z[g_place(t), o, 0].astype(jnp.float32) * weights[o : o + 1, :]
                whole = whole + g_z[g_place(t), o, 1].astype(jnp.float32)
            g_red[g_place(t)] = whole.astype(jnp.bfloat16)
            loop(0, nz - 1, lambda e: back_copy(t, e).start())
            g_final[g_part(t)] = whole.astype(jnp.bfloat16)

    def interleave(tile):
        down = lax.broadcasted_iota(jnp.int32, (SUB, LANES), 0)
        across = lax.broadcasted_iota(jnp.int32, (SUB, LANES), 1)
        index = down * (LANES // SUB) + across // SUB
        mixed = jnp.zeros((SUB, LANES), jnp.float32)
        for j in range(SUB):
            row = jnp.broadcast_to(tile[j : j + 1, :], (SUB, LANES))
            row = jnp.take_along_axis(row, index, axis=1, mode="promise_in_bounds")
            mixed = jnp.where(across % SUB == j, row, mixed)
        return mixed

    loop(0, CHIPS - 1, lambda s: c_chip_copy(s).wait_recv())
    loop(0, CHIPS, lambda s: c_beside_copy(s).wait_recv())
    c_total = c_send[CHIPS - 1, half_at(odd), :]
    for s in range(2 * CHIPS):
        if s != CHIPS - 1:
            c_total = c_total + c_block[s]

    def c_many_copy(e):
        to = along(lax.rem(pair + hop(e, pairs), pairs) * 2 + odd)
        return copy(c_half, c_many.at[pair], cz_sems.at[0, e], cz_sems.at[1, e], to)

    c_half[...] = c_total
    c_many[pair] = c_total
    loop(0, pairs - 1, lambda e: c_many_copy(e).start())

    def c_final_at(side, place):
        return c_fin.at[pl.ds(pl.multiple_of((side * CHIPS + place) * 2 * C_ROWS, 8), 2 * C_ROWS)]

    c_final = c_final_at(core, x * NY + y)
    def g_at(side, s):
        from_x, from_y = chip_at(s, -1)
        return g_fin.at[from_x, side, from_y]

    def g_out(s):
        return copy(g_final, g_final, gf_sems.at[0, s], gf_sems.at[1, s], chip(s))

    def g_in(s):
        return copy(g_at(core, s), g_at(core, s), gf_sems.at[0, s], gf_sems.at[1, s], chip(s))

    def g_row(side, a):
        return g_fin.at[x_at(a, -1), side]

    def g_share(a):
        return copy(g_row(core, a), g_row(core, a), gs_sems.at[0, a], gs_sems.at[1, a], sibling)

    def g_shared(a):
        return copy(g_row(other, a), g_row(other, a), gs_sems.at[0, a], gs_sems.at[1, a], sibling)

    def c_out(s):
        mine = c_final.at[half_at(odd)]
        return copy(mine, mine, cf_sems.at[0, s], cf_sems.at[1, s], chip(s))

    def c_out_beside(s):
        mine = c_final.at[half_at(odd)]
        return copy(mine, mine, cf_sems.at[0, CHIPS + s], cf_sems.at[1, CHIPS + s], chip_beside(s))

    def c_at(side, s):
        return c_final_at(side, place_at(s, -1))

    def c_in(s):
        came = c_at(core, s).at[half_at(odd)]
        return copy(came, came, cf_sems.at[0, s], cf_sems.at[1, s], chip(s))

    def c_in_beside(s):
        came = c_at(core, s).at[half_at(1 - odd)]
        return copy(came, came, cf_sems.at[0, CHIPS + s], cf_sems.at[1, CHIPS + s], chip(s))

    def c_row(side, a):
        first = (side * CHIPS + x_at(a, -1) * NY) * 2 * C_ROWS
        return c_fin.at[pl.ds(pl.multiple_of(first, 8), NY * 2 * C_ROWS)]

    def c_share(a):
        return copy(c_row(core, a), c_row(core, a), cs_sems.at[0, a], cs_sems.at[1, a], sibling)

    def c_shared(a):
        return copy(c_row(other, a), c_row(other, a), cs_sems.at[0, a], cs_sems.at[1, a], sibling)

    for t in range(TILES):

        @pl.when(z != g_owner(t))
        def _(t=t):
            back_copy(t, 0).wait_recv()

    loop(0, CHIPS - 1, lambda s: g_out(s).start())
    loop(0, pairs - 1, lambda e: c_many_copy(e).wait_recv())
    c_total = c_many[0]
    for o in range(1, pairs):
        c_total = c_total + c_many[o]
    first = pl.multiple_of(odd * C_ROWS, 8)
    for i in range(C_SUBS):
        c_final[pl.ds(pl.multiple_of(first + i * SUB, 8), SUB), :] = interleave(
            c_total[i * SUB : (i + 1) * SUB]
        )


    def c_spread(s):
        c_out_beside(s).start()
        c_out(s).start()

    loop(0, CHIPS - 1, c_spread)
    c_out_beside(CHIPS - 1).start()

    def pass_on(came, share):
        def act(a):
            loop(a * NY, min(a * NY + NY, CHIPS - 1), lambda s: came(s).wait_recv())
            share(a).start()

        loop(0, NX, act)

    pass_on(g_in, g_share)
    loop(1, NX, lambda d: q_copy(d).wait_recv())
    loop(0, NX, lambda a: g_shared(a).wait_recv())
    total = jnp.zeros((HEAD_ROWS, D), jnp.float32)
    for o in range(NX):
        total = total + lax.dot_general(
            q_all[o], g_fin[o].reshape(D, Q_DEV), NT, preferred_element_type=jnp.float32
        )
    head[...] = total

    def c_pass(a):
        loop(a * NY, min(a * NY + NY, CHIPS - 1), lambda s: c_in(s).wait_recv())
        loop(a * NY, a * NY + NY, lambda s: c_in_beside(s).wait_recv())
        c_share(a).start()

    loop(0, NX, c_pass)
    loop(0, NX, lambda a: c_shared(a).wait_recv())
    for u in range(2 * SUB):
        out[:, u * LANES : (u + 1) * LANES] = c_fin[pl.ds(u, M, stride=2 * SUB), :]

    loop(1, NEAR, lambda d: near_copy(d).wait_send())
    loop(0, nz - 1, lambda e: far_copy(e).wait_send())
    loop(1, NX, lambda d: q_copy(d).wait_send())
    g_core_copy().wait_send()
    loop(0, NX, lambda a: c_core_copy(a).wait_send())
    loop(1, NY, lambda d: g_y_copy(d).wait_send())
    loop(0, CHIPS - 1, lambda s: c_chip_copy(s).wait_send())
    for t in range(TILES):

        @pl.when(z == g_owner(t))
        def _(t=t):
            loop(0, nz - 1, lambda e: back_copy(t, e).wait_send())

        @pl.when(z != g_owner(t))
        def _(t=t):
            z_copy(t).wait_send()

    loop(0, CHIPS, lambda s: c_beside_copy(s).wait_send())
    loop(0, pairs - 1, lambda e: c_many_copy(e).wait_send())
    loop(0, CHIPS - 1, lambda s: g_out(s).wait_send())
    loop(0, NX, lambda a: g_share(a).wait_send())
    loop(0, CHIPS - 1, lambda s: c_out(s).wait_send())
    loop(0, CHIPS, lambda s: c_out_beside(s).wait_send())
    loop(0, NX, lambda a: c_share(a).wait_send())


def finish_kernel(loss_in, head_in, book_in, loss_out, head_out, book_out, sems):
    moves = [(loss_in, loss_out)]
    for i in range(3):
        rows = pl.ds(i * (M // 3), M // 3)
        moves.append((book_in.at[rows], book_out.at[rows]))
    for i in range(2):
        rows = pl.ds(i * (HEAD_ROWS // 2), HEAD_ROWS // 2)
        moves.append((head_in.at[rows], head_out.at[rows]))
    copies = [pltpu.make_async_copy(src, dst, sems.at[i]) for i, (src, dst) in enumerate(moves)]
    for each in copies:
        each.start()
    for each in copies:
        each.wait()


def step(nz, queries_in, head_weight, codebook, codes, slab_sizes, positive_ids):
    left = pl.BlockSpec(memory_space=pltpu.HBM)
    whole = pl.BlockSpec(memory_space=pltpu.VMEM)
    dma = pltpu.SemaphoreType.DMA
    f32, bf16 = jnp.float32, jnp.bfloat16
    per = -(-TILES // nz)
    outs = [(1, Q_DEV), (HEAD_ROWS, D), (M, K * SUB)]
    ins = [positive_ids.reshape(1, Q_DEV), queries_in, head_weight, codebook, codes.T]
    ins = [pltpu.with_memory_space_constraint(each, pltpu.HBM) for each in ins]
    loss, head_grad, book = pl.pallas_call(
        functools.partial(step_kernel, nz),
        out_shape=[pltpu.VMEM(shape, f32) for shape in outs],
        in_specs=[pl.BlockSpec(memory_space=pltpu.SMEM)] + [left] * 5,
        out_specs=[whole] * 3,
        scratch_shapes=[
            pltpu.VMEM((1, Q_DEV), jnp.int32),
            pltpu.VMEM((Q_DEV, D), bf16),
            pltpu.VMEM((D, D), bf16),
            pltpu.VMEM((M, K * SUB), bf16),
            pltpu.VMEM((M, SLOT_DEV), jnp.int32),
            pltpu.VMEM((2 * D, LANES), f32),
            pltpu.VMEM((D, SLOT_DEV), bf16),
            pltpu.VMEM((D, Q_DEV), bf16),
            pltpu.VMEM((D, Q_DEV), bf16),
            pltpu.VMEM((D, SLOT_DEV), f32),
            pltpu.VMEM((8, Q_DEV), f32),
            pltpu.VMEM((NEAR, 8, Q_DEV), f32),
            pltpu.VMEM((nz, 8, Q_DEV), f32),
            pltpu.VMEM((8, Q_DEV), f32),
            pltpu.VMEM((D, K), f32),
            pltpu.VMEM((Q_DEV, SLOT_DEV), bf16),
            pltpu.VMEM((D, 2 * Q_DEV), f32),
            pltpu.VMEM((M * Q_DEV, K), bf16),
            pltpu.VMEM((D, K), f32),
            pltpu.VMEM((D, Q_DEV), f32),
            pltpu.VMEM((NX, HEAD_ROWS, Q_DEV), bf16),
            pltpu.VMEM((D // 16, 2, 16, Q_DEV), bf16),
            pltpu.VMEM((HALF // 16, 2, 16, Q_DEV), bf16),
            pltpu.VMEM((NY, TILES, 2, 16, Q_DEV), bf16),
            pltpu.VMEM((NY, TILES, 2, 16, Q_DEV), bf16),
            pltpu.VMEM((TILES, 2, 16, Q_DEV), bf16),
            pltpu.VMEM((per, nz, 2, 16, Q_DEV), bf16),
            pltpu.VMEM((per, 16, Q_DEV), bf16),
            pltpu.VMEM((NX, 2, NY, G_ROWS, Q_DEV), bf16),
            pltpu.VMEM((NX, NY * C_ROWS, K), f32),
            pltpu.VMEM((CHIPS, 2 * C_ROWS, LANES), f32),
            pltpu.VMEM((2 * CHIPS, C_ROWS, LANES), f32),
            pltpu.VMEM((C_ROWS, LANES), f32),
            pltpu.VMEM((nz // 2, C_ROWS, LANES), f32),
            pltpu.VMEM((2 * D, LANES), f32),
            dma((5,)),
            dma((2, NEAR)),
            dma((2, nz)),
            dma((2, NX)),
            dma((2,)),
            dma((2, NY)),
            dma((TILES,)),
            dma((per, nz)),
            dma((per, nz)),
            dma((TILES,)),
            dma((2, CHIPS)),
            dma((2, NX)),
            dma((2, NX)),
            dma((2, 2 * CHIPS)),
            dma((2, nz // 2)),
            dma((2, 2 * CHIPS)),
            dma((2, NX)),
        ],
        compiler_params=pltpu.CompilerParams(
            collective_id=0, has_side_effects=True, vmem_limit_bytes=VMEM_BYTES
        ),
    )(slab_sizes, *ins)
    loss, head_grad, book = pl.pallas_call(
        finish_kernel,
        out_shape=[jax.ShapeDtypeStruct(shape, f32) for shape in outs],
        in_specs=[whole] * 3,
        out_specs=[left] * 3,
        scratch_shapes=[dma((6,))],
        compiler_params=pltpu.CompilerParams(vmem_limit_bytes=VMEM_BYTES),
    )(loss, head_grad, book)
    return loss.reshape(Q_DEV), head_grad, book


def solution(mesh):
    nz = mesh.shape["corpus"] // (2 * NY)
    return jax.shard_map(
        functools.partial(step, nz),
        mesh=mesh,
        in_specs=(P("query", None), P(), P(), P("corpus", None), P("corpus"), P("query")),
        out_specs=(P("query"), P("query", None), P()),
        check_vma=False,
    )
```

```python
import functools

import jax
import jax.numpy as jnp
from jax import lax
from jax.experimental import pallas as pl
from jax.experimental.pallas import tpu as pltpu
from jax.sharding import PartitionSpec as P

D = 768
M = 96
K = 256
SUB = 8
SLOT_DEV = 384
Q_DEV = 128
LANES = 128
NX = 4
NY = 4
CHIPS = NX * NY
HALF = D // 2
G_ROWS = HALF // NY
C_ROWS = HALF // CHIPS
C_SUBS = C_ROWS // SUB
HEAD_ROWS = D // NX
TILES = 6
G_TILE = G_ROWS // TILES
NEAR = 2 * NY
MESH = pl.DeviceIdType.MESH
NT = (((1,), (1,)), ((), ()))
VMEM_BYTES = 48 * 1024 * 1024


def loop(start, count, act):
    if isinstance(start, int) and isinstance(count, int):
        for step in range(start, count):
            act(step)
        return
    def body(step, carry):
        act(step)
        return carry

    lax.fori_loop(start, count, body, 0)


def spread(a):
    return 2 - a + 3 * (a // 2) - 2 * (a // 3)


def step_kernel(
    nz,
    length_ref, ids_hbm, qin_hbm, weight_hbm, codebook_hbm, codes_hbm,
    loss, head, out,
    ids, qin, weight, codebook, codes, table, pt, qt, qint, pgt, stats, near, far, mid, book,
    pu, sides, mass, fixed, scaled,
    q_all, grad, g_core, g_send, g_block, g_sum, g_z, g_red, g_fin,
    c_core, c_send, c_block, c_half, c_many, c_fin,
    in_sems, near_sems, far_sems,
    q_sems, gc_sems, gy_sems, gz_send, gz_recv, gr_send, gr_recv, gf_sems, gs_sems,
    cc_sems, cy_sems, cz_sems, cf_sems, cs_sems,
):
    me = lax.axis_index("corpus")
    x, y, z, core = lax.axis_index("query"), me // (2 * nz), lax.rem(me // 2, nz), lax.rem(me, 2)
    other = 1 - core
    group = y * 2 + core

    def device(to_x, to_y, to_z, to_core):
        return {"corpus": (to_y * nz + to_z) * 2 + to_core, "query": to_x}

    sibling = device(x, y, z, other)

    def around(o):
        return device(x, o // 2, z, lax.rem(o, 2))

    def along(o):
        return device(x, y, o, core)

    def hop(e, ring=nz):
        return ring // 2 + ((e + 1) // 2) * (1 - 2 * (e % 2))

    def chip_at(s, sign):
        to_x = lax.rem(x + 4 + sign * spread(s // 4), NX)
        to_y = lax.rem(y + 4 + sign * spread(s % 4), NY)
        return to_x, to_y

    def place_at(s, sign):
        to_x, to_y = chip_at(s, sign)
        return to_x * NY + to_y

    def chip(s, sign=1):
        to_x, to_y = chip_at(s, sign)
        return device(to_x, to_y, z, core)

    odd, pair, pairs = lax.rem(z, 2), z // 2, nz // 2

    def chip_beside(s):
        to_x, to_y = chip_at(s, 1)
        return device(to_x, to_y, z + 1 - 2 * odd, core)

    def half_at(which):
        return pl.ds(pl.multiple_of(which * C_ROWS, 8), C_ROWS)

    def y_at(d):
        return lax.rem(y + d, NY)

    def copy(src, dst, send, recv, to):
        return pltpu.make_async_remote_copy(
            src_ref=src, dst_ref=dst, send_sem=send, recv_sem=recv, device_id=to, device_id_type=MESH
        )

    barrier = pltpu.get_barrier_semaphore()

    def greet(to):
        pl.semaphore_signal(barrier, 1, device_id=to, device_id_type=MESH)

    loop(0, nz - 1, lambda e: greet(along(lax.rem(z + hop(e), nz))))
    loads = [
        pltpu.make_async_copy(src, dst, in_sems.at[i])
        for i, (src, dst) in enumerate(
            [(codebook_hbm, codebook), (codes_hbm, codes), (qin_hbm, qin), (weight_hbm, weight), (ids_hbm, ids)]
        )
    ]
    for load in loads:
        load.start()
    loop(1, NEAR, lambda d: greet(around(lax.rem(group + d, NEAR))))
    loop(0, 12, lambda s: greet(chip(s)))
    loop(0, CHIPS - 1, lambda s: greet(chip_beside(s)))

    wide = K * SUB // 2
    down = lax.broadcasted_iota(jnp.int32, (wide, wide), 0)
    across = lax.broadcasted_iota(jnp.int32, (wide, wide), 1)
    pick = down == (across % LANES) * SUB + across // LANES
    pick = jnp.where(pick, jnp.float32(1), jnp.float32(0)).astype(jnp.bfloat16)
    loads[0].wait()
    for part in range(2):
        words = jnp.dot(
            codebook[:, part * wide : (part + 1) * wide], pick, preferred_element_type=jnp.float32
        )
        for j in range(SUB):
            table[pl.ds(part * D + j, M, stride=SUB), :] = words[:, j * LANES : (j + 1) * LANES]
    loads[1].wait()

    def rebuild(pair, carry):
        halves = []
        for part in range(2):
            m = pair * 2 + part
            lower = table[pl.ds(pl.multiple_of(m * SUB, SUB), SUB), :]
            upper = table[pl.ds(pl.multiple_of(D + m * SUB, SUB), SUB), :]
            row = codes[pl.ds(m, 1), :]
            parts = []
            for tile in range(SLOT_DEV // LANES):
                index = jnp.broadcast_to(row[:, tile * LANES : (tile + 1) * LANES], (SUB, LANES))
                low = index & (LANES - 1)
                first = jnp.take_along_axis(lower, low, axis=1, mode="promise_in_bounds")
                second = jnp.take_along_axis(upper, low, axis=1, mode="promise_in_bounds")
                parts.append(jnp.where(index >= LANES, second, first))
            halves.append(jnp.concatenate(parts, axis=1))
        rows = jnp.concatenate(halves, axis=0).astype(jnp.bfloat16)
        pt[pl.ds(pl.multiple_of(pair * 2 * SUB, 2 * SUB), 2 * SUB), :] = rows
        return carry

    lax.fori_loop(0, M // 2, rebuild, 0, unroll=4)

    loads[2].wait()
    loads[3].wait()
    loads[4].wait()
    query = jnp.dot(qin[...], weight[...], preferred_element_type=jnp.float32).astype(jnp.bfloat16)
    scores = jnp.dot(query, pt[...], preferred_element_type=jnp.float32).T
    slot = lax.broadcasted_iota(jnp.int32, (SLOT_DEV, Q_DEV), 0)
    scores = jnp.where(slot < length_ref[0], scores, -jnp.inf)
    owned = slot == ids[...] - me * SLOT_DEV
    peak = jnp.max(scores, axis=0, keepdims=True)
    raised = jnp.exp(scores - peak)
    total = jnp.sum(raised, axis=0, keepdims=True)
    positive = jnp.sum(jnp.where(owned, scores, 0.0), axis=0, keepdims=True)
    pad = jnp.zeros((5, Q_DEV), jnp.float32)
    stats[...] = jnp.concatenate([peak, total, positive, pad], axis=0)
    pl.semaphore_wait(barrier, NEAR - 1 + nz - 1 + 12 + CHIPS - 1)

    def merge(slots):
        peaks, totals, positives = slots[:, 0, :], slots[:, 1, :], slots[:, 2, :]
        peak = jnp.max(peaks, axis=0, keepdims=True)
        total = jnp.sum(totals * jnp.exp(peaks - peak), axis=0, keepdims=True)
        return peak, total, jnp.sum(positives, axis=0, keepdims=True)

    def near_copy(d):
        to = around(lax.rem(group + d, NEAR))
        return copy(stats, near.at[group], near_sems.at[0, d], near_sems.at[1, d], to)

    def far_copy(e):
        to = along(lax.rem(z + hop(e), nz))
        return copy(mid, far.at[z], far_sems.at[0, e], far_sems.at[1, e], to)

    def q_copy(d):
        to = lax.rem(x + d, NX)
        rows = pl.ds(pl.multiple_of(to * HEAD_ROWS, 16), HEAD_ROWS)
        return copy(qint.at[rows], q_all.at[x], q_sems.at[0, d], q_sems.at[1, d], device(to, y, z, core))

    def onto(m):
        rows = pl.ds(pl.multiple_of(m * SUB, SUB), SUB)
        part = pgt[rows, :]
        upper = part.astype(jnp.bfloat16)
        lower = (part - upper.astype(jnp.float32)).astype(jnp.bfloat16)
        code = codes[pl.ds(m, 1), :].astype(jnp.float32).astype(jnp.bfloat16)
        onehot = jnp.where(word == code, jnp.bfloat16(1), jnp.bfloat16(0))
        left = jnp.concatenate([pu[...], upper, lower], axis=0)
        sums = lax.dot_general(left, onehot, NT, preferred_element_type=jnp.float32)
        mass[pl.ds(pl.multiple_of(m * Q_DEV, Q_DEV), Q_DEV), :] = sums[:Q_DEV].astype(jnp.bfloat16)
        fixed[rows, :] = sums[Q_DEV : Q_DEV + SUB] + sums[Q_DEV + SUB :]

    def onto_range(first, last):
        def body(m, carry):
            onto(m)
            return carry

        lax.fori_loop(first, last, body, 0, unroll=4)

    def g_core_copy():
        rows = pl.ds(other * (HALF // 16), HALF // 16)
        return copy(grad.at[rows], g_core, gc_sems.at[0], gc_sems.at[1], sibling)

    def g_y_copy(d):
        to = device(x, y_at(d), z, core)
        return copy(g_send.at[d], g_block.at[d], gy_sems.at[0, d], gy_sems.at[1, d], to)

    def g_pair(d):
        first = y_at(d) * TILES
        mine = grad[pl.ds(core * (HALF // 16) + first, TILES)].astype(jnp.float32)
        theirs = g_core[pl.ds(first, TILES)].astype(jnp.float32)
        soft = mine[:, 0] * jnp.exp(peak - near_peak) + theirs[:, 0] * jnp.exp(sibling_peak - near_peak)
        return soft, mine[:, 1] + theirs[:, 1]

    def g_go(d):
        soft, rows = g_pair(d)
        g_send[d, :, 0] = soft.astype(jnp.bfloat16)
        g_send[d, :, 1] = rows.astype(jnp.bfloat16)
        g_y_copy(d).start()

    loop(1, NEAR, lambda d: near_copy(d).start())
    near[group] = stats[...]
    qt[...] = query.astype(jnp.float32).T.astype(jnp.bfloat16)
    qint[...] = qin[...].astype(jnp.float32).T.astype(jnp.bfloat16)
    pu[...] = raised.T.astype(jnp.bfloat16)
    minus = jnp.where(owned, -1.0, 0.0).astype(jnp.bfloat16)
    both = jnp.concatenate([raised.astype(jnp.bfloat16), minus], axis=1)
    sides[...] = jnp.dot(pt[...], both, preferred_element_type=jnp.float32)

    tiles = (D // 16, 16, Q_DEV)
    grad[:, 0] = sides[:, :Q_DEV].astype(jnp.bfloat16).reshape(tiles)
    grad[:, 1] = sides[:, Q_DEV:].astype(jnp.bfloat16).reshape(tiles)
    g_core_copy().start()
    pgt[...] = lax.dot_general(qt[...], minus, NT, preferred_element_type=jnp.float32)
    word = lax.broadcasted_iota(jnp.int32, (K, SLOT_DEV), 0).astype(jnp.float32)
    word = word.astype(jnp.bfloat16)
    onto_range(0, 20)
    loop(1, NEAR, lambda d: near_copy(d).wait_recv())
    near_peak, near_total, near_positive = merge(near[...])
    mid[...] = jnp.concatenate([near_peak, near_total, near_positive, pad], axis=0)
    loop(0, nz - 1, lambda e: far_copy(e).start())
    far[z] = mid[...]

    sibling_peak = near[y * 2 + other, 0:1, :]
    g_core_copy().wait_recv()
    loop(1, NY, g_go)
    loop(1, NX, lambda d: q_copy(d).start())
    q_all[x] = qint[pl.ds(pl.multiple_of(x * HEAD_ROWS, 16), HEAD_ROWS), :]
    onto_range(20, 60)

    def g_part(t):
        return (pl.ds(t * G_TILE, G_TILE), slice(None))

    def g_owner(t):
        return (t * nz) // TILES

    def g_place(t):
        return sum(1 for s in range(t) if g_owner(s) == g_owner(t))

    def z_copy(t):
        p = g_place(t)
        return copy(g_sum.at[t], g_z.at[p, z], gz_send.at[t], gz_recv.at[p, z], along(g_owner(t)))

    def z_heard(t, o):
        p = g_place(t)
        return copy(g_z.at[p, o], g_z.at[p, o], gz_send.at[t], gz_recv.at[p, o], along(o))

    g_final = g_fin.at[x, core, y]

    def back_copy(t, e):
        to = along(lax.rem(z + hop(e), nz))
        return copy(g_red.at[g_place(t)], g_final.at[g_part(t)], gr_send.at[g_place(t), e], gr_recv.at[t], to)

    loop(1, NY, lambda d: g_y_copy(d).wait_recv())
    soft, rows = g_pair(0)
    for d in range(1, NY):
        soft = soft + g_block[d, :, 0].astype(jnp.float32)
        rows = rows + g_block[d, :, 1].astype(jnp.float32)
    g_sum[:, 0] = soft.astype(jnp.bfloat16)
    g_sum[:, 1] = rows.astype(jnp.bfloat16)
    for t in range(TILES):

        @pl.when(z == g_owner(t))
        def _(t=t):
            g_z[g_place(t), z] = g_sum[t]

        @pl.when(z != g_owner(t))
        def _(t=t):
            z_copy(t).start()

    onto_range(60, M)
    loop(0, nz - 1, lambda e: far_copy(e).wait_recv())
    last_peak, total, positive = merge(far[...])
    log_total = last_peak + jnp.log(total)
    loss[...] = log_total - positive
    scaled[...] = qt[...].astype(jnp.float32) * jnp.exp(peak - log_total)

    def split(m):
        part = scaled[pl.ds(pl.multiple_of(m * SUB, SUB), SUB), :]
        upper = part.astype(jnp.bfloat16)
        lower = (part - upper.astype(jnp.float32)).astype(jnp.bfloat16)
        return jnp.concatenate([upper, lower], axis=0)

    def x_at(a, sign=1):
        return lax.rem(x + 4 + sign * spread(a), NX)

    def c_compute(side, a):
        for i in range(0, NY * C_SUBS, 2):
            m = side * (M // 2) + x_at(a) * (NY * C_SUBS) + i
            nil = jnp.zeros((2 * SUB, Q_DEV), jnp.bfloat16)
            first = jnp.concatenate([split(m), nil], axis=1)
            second = jnp.concatenate([nil, split(m + 1)], axis=1)
            both_of = mass[pl.ds(pl.multiple_of(m * Q_DEV, Q_DEV), 2 * Q_DEV), :]
            sums = jnp.dot(
                jnp.concatenate([first, second], axis=0), both_of, preferred_element_type=jnp.float32
            )
            rows = pl.ds(pl.multiple_of(m * SUB, SUB), 2 * SUB)
            sums = [sums[k * SUB : (k + 1) * SUB] for k in range(4)]
            book[rows, :] = jnp.concatenate([sums[0] + sums[1], sums[2] + sums[3]], axis=0) + fixed[rows, :]

    def c_core_copy(a):
        rows = pl.ds(pl.multiple_of(other * HALF + x_at(a) * NY * C_ROWS, 8), NY * C_ROWS)
        return copy(book.at[rows], c_core.at[a], cc_sems.at[0, a], cc_sems.at[1, a], sibling)

    def c_chip_copy(s):
        return copy(
            c_send.at[s, half_at(odd)], c_block.at[s], cy_sems.at[0, s], cy_sems.at[1, s], chip(s)
        )

    def c_beside_copy(s):
        k = CHIPS + s
        return copy(
            c_send.at[s, half_at(1 - odd)], c_block.at[k], cy_sems.at[0, k], cy_sems.at[1, k], chip_beside(s)
        )

    def c_add(s):
        to_x, to_y = chip_at(s, 1)
        rows = pl.ds(pl.multiple_of(core * HALF + (to_x * NY + to_y) * C_ROWS, 8), C_ROWS)
        there = pl.ds(pl.multiple_of(to_y * C_ROWS, 8), C_ROWS)
        both = book[rows, :] + c_core[s // NY, there, :]
        for i in range(C_SUBS):
            for part in range(2):
                tile = both[i * SUB : (i + 1) * SUB, part * LANES : (part + 1) * LANES]
                c_send[s, pl.ds((2 * i + part) * SUB, SUB), :] = tile

    def c_go(s):
        c_add(s)
        c_beside_copy(s).start()
        c_chip_copy(s).start()

    def c_near(a):
        c_compute(other, a)
        c_core_copy(a).start()

    def c_away(a, count):
        c_compute(core, a)
        c_core_copy(a).wait_recv()
        loop(a * NY, a * NY + count, c_go)

    loop(0, NX, c_near)
    loop(0, NX - 1, lambda a: c_away(a, NY))
    c_away(NX - 1, NY - 1)
    c_add(CHIPS - 1)
    c_beside_copy(CHIPS - 1).start()

    for t in range(TILES):

        @pl.when(z == g_owner(t))
        def _(t=t):
            loop(0, nz - 1, lambda e: z_heard(t, lax.rem(z + hop(e), nz)).wait_recv())
            weights = jnp.exp(far[...][:, 0, :] - log_total)
            whole = jnp.zeros((16, Q_DEV), jnp.float32)
            for o in range(nz):
                whole = whole + g_z[g_place(t), o, 0].astype(jnp.float32) * weights[o : o + 1, :]
                whole = whole + g_z[g_place(t), o, 1].astype(jnp.float32)
            g_red[g_place(t)] = whole.astype(jnp.bfloat16)
            loop(0, nz - 1, lambda e: back_copy(t, e).start())
            g_final[g_part(t)] = whole.astype(jnp.bfloat16)

    def interleave(tile):
        down = lax.broadcasted_iota(jnp.int32, (SUB, LANES), 0)
        across = lax.broadcasted_iota(jnp.int32, (SUB, LANES), 1)
        index = down * (LANES // SUB) + across // SUB
        mixed = jnp.zeros((SUB, LANES), jnp.float32)
        for j in range(SUB):
            row = jnp.broadcast_to(tile[j : j + 1, :], (SUB, LANES))
            row = jnp.take_along_axis(row, index, axis=1, mode="promise_in_bounds")
            mixed = jnp.where(across % SUB == j, row, mixed)
        return mixed

    loop(0, CHIPS - 1, lambda s: c_chip_copy(s).wait_recv())
    loop(0, CHIPS, lambda s: c_beside_copy(s).wait_recv())
    c_total = c_send[CHIPS - 1, half_at(odd), :]
    for s in range(2 * CHIPS):
        if s != CHIPS - 1:
            c_total = c_total + c_block[s]

    def c_many_copy(e):
        to = along(lax.rem(pair + hop(e, pairs), pairs) * 2 + odd)
        return copy(c_half, c_many.at[pair], cz_sems.at[0, e], cz_sems.at[1, e], to)

    c_half[...] = c_total
    c_many[pair] = c_total
    loop(0, pairs - 1, lambda e: c_many_copy(e).start())

    def c_final_at(side, place):
        return c_fin.at[pl.ds(pl.multiple_of((side * CHIPS + place) * 2 * C_ROWS, 8), 2 * C_ROWS)]

    c_final = c_final_at(core, x * NY + y)
    def g_at(side, s):
        from_x, from_y = chip_at(s, -1)
        return g_fin.at[from_x, side, from_y]

    def g_out(s):
        return copy(g_final, g_final, gf_sems.at[0, s], gf_sems.at[1, s], chip(s))

    def g_in(s):
        return copy(g_at(core, s), g_at(core, s), gf_sems.at[0, s], gf_sems.at[1, s], chip(s))

    def g_row(side, a):
        return g_fin.at[x_at(a, -1), side]

    def g_share(a):
        return copy(g_row(core, a), g_row(core, a), gs_sems.at[0, a], gs_sems.at[1, a], sibling)

    def g_shared(a):
        return copy(g_row(other, a), g_row(other, a), gs_sems.at[0, a], gs_sems.at[1, a], sibling)

    def c_out(s):
        mine = c_final.at[half_at(odd)]
        return copy(mine, mine, cf_sems.at[0, s], cf_sems.at[1, s], chip(s))

    def c_out_beside(s):
        mine = c_final.at[half_at(odd)]
        return copy(mine, mine, cf_sems.at[0, CHIPS + s], cf_sems.at[1, CHIPS + s], chip_beside(s))

    def c_at(side, s):
        return c_final_at(side, place_at(s, -1))

    def c_in(s):
        came = c_at(core, s).at[half_at(odd)]
        return copy(came, came, cf_sems.at[0, s], cf_sems.at[1, s], chip(s))

    def c_in_beside(s):
        came = c_at(core, s).at[half_at(1 - odd)]
        return copy(came, came, cf_sems.at[0, CHIPS + s], cf_sems.at[1, CHIPS + s], chip(s))

    def c_row(side, a):
        first = (side * CHIPS + x_at(a, -1) * NY) * 2 * C_ROWS
        return c_fin.at[pl.ds(pl.multiple_of(first, 8), NY * 2 * C_ROWS)]

    def c_share(a):
        return copy(c_row(core, a), c_row(core, a), cs_sems.at[0, a], cs_sems.at[1, a], sibling)

    def c_shared(a):
        return copy(c_row(other, a), c_row(other, a), cs_sems.at[0, a], cs_sems.at[1, a], sibling)

    for t in range(TILES):

        @pl.when(z != g_owner(t))
        def _(t=t):
            back_copy(t, 0).wait_recv()

    loop(0, CHIPS - 1, lambda s: g_out(s).start())
    loop(0, pairs - 1, lambda e: c_many_copy(e).wait_recv())
    c_total = c_many[0]
    for o in range(1, pairs):
        c_total = c_total + c_many[o]
    first = pl.multiple_of(odd * C_ROWS, 8)
    for i in range(C_SUBS):
        c_final[pl.ds(pl.multiple_of(first + i * SUB, 8), SUB), :] = interleave(
            c_total[i * SUB : (i + 1) * SUB]
        )


    def c_spread(s):
        c_out_beside(s).start()
        c_out(s).start()

    loop(0, CHIPS - 1, c_spread)
    c_out_beside(CHIPS - 1).start()

    def pass_on(came, share):
        def act(a):
            loop(a * NY, min(a * NY + NY, CHIPS - 1), lambda s: came(s).wait_recv())
            share(a).start()

        loop(0, NX, act)

    pass_on(g_in, g_share)
    loop(1, NX, lambda d: q_copy(d).wait_recv())
    loop(0, NX, lambda a: g_shared(a).wait_recv())
    total = jnp.zeros((HEAD_ROWS, D), jnp.float32)
    for o in range(NX):
        total = total + lax.dot_general(
            q_all[o], g_fin[o].reshape(D, Q_DEV), NT, preferred_element_type=jnp.float32
        )
    head[...] = total

    def c_pass(a):
        loop(a * NY, min(a * NY + NY, CHIPS - 1), lambda s: c_in(s).wait_recv())
        loop(a * NY, a * NY + NY, lambda s: c_in_beside(s).wait_recv())
        c_share(a).start()

    loop(0, NX, c_pass)
    loop(0, NX, lambda a: c_shared(a).wait_recv())
    for u in range(2 * SUB):
        out[:, u * LANES : (u + 1) * LANES] = c_fin[pl.ds(u, M, stride=2 * SUB), :]

    loop(1, NEAR, lambda d: near_copy(d).wait_send())
    loop(0, nz - 1, lambda e: far_copy(e).wait_send())
    loop(1, NX, lambda d: q_copy(d).wait_send())
    g_core_copy().wait_send()
    loop(0, NX, lambda a: c_core_copy(a).wait_send())
    loop(1, NY, lambda d: g_y_copy(d).wait_send())
    loop(0, CHIPS - 1, lambda s: c_chip_copy(s).wait_send())
    for t in range(TILES):

        @pl.when(z == g_owner(t))
        def _(t=t):
            loop(0, nz - 1, lambda e: back_copy(t, e).wait_send())

        @pl.when(z != g_owner(t))
        def _(t=t):
            z_copy(t).wait_send()

    loop(0, CHIPS, lambda s: c_beside_copy(s).wait_send())
    loop(0, pairs - 1, lambda e: c_many_copy(e).wait_send())
    loop(0, CHIPS - 1, lambda s: g_out(s).wait_send())
    loop(0, NX, lambda a: g_share(a).wait_send())
    loop(0, CHIPS - 1, lambda s: c_out(s).wait_send())
    loop(0, CHIPS, lambda s: c_out_beside(s).wait_send())
    loop(0, NX, lambda a: c_share(a).wait_send())


def finish_kernel(loss_in, head_in, book_in, loss_out, head_out, book_out, sems):
    moves = [(loss_in, loss_out)]
    for i in range(3):
        rows = pl.ds(i * (M // 3), M // 3)
        moves.append((book_in.at[rows], book_out.at[rows]))
    for i in range(2):
        rows = pl.ds(i * (HEAD_ROWS // 2), HEAD_ROWS // 2)
        moves.append((head_in.at[rows], head_out.at[rows]))
    copies = [pltpu.make_async_copy(src, dst, sems.at[i]) for i, (src, dst) in enumerate(moves)]
    for each in copies:
        each.start()
    for each in copies:
        each.wait()


def step(nz, queries_in, head_weight, codebook, codes, slab_sizes, positive_ids):
    left = pl.BlockSpec(memory_space=pltpu.HBM)
    whole = pl.BlockSpec(memory_space=pltpu.VMEM)
    dma = pltpu.SemaphoreType.DMA
    f32, bf16 = jnp.float32, jnp.bfloat16
    per = -(-TILES // nz)
    outs = [(1, Q_DEV), (HEAD_ROWS, D), (M, K * SUB)]
    ins = [positive_ids.reshape(1, Q_DEV), queries_in, head_weight, codebook, codes.T]
    ins = [pltpu.with_memory_space_constraint(each, pltpu.HBM) for each in ins]
    loss, head_grad, book = pl.pallas_call(
        functools.partial(step_kernel, nz),
        out_shape=[pltpu.VMEM(shape, f32) for shape in outs],
        in_specs=[pl.BlockSpec(memory_space=pltpu.SMEM)] + [left] * 5,
        out_specs=[whole] * 3,
        scratch_shapes=[
            pltpu.VMEM((1, Q_DEV), jnp.int32),
            pltpu.VMEM((Q_DEV, D), bf16),
            pltpu.VMEM((D, D), bf16),
            pltpu.VMEM((M, K * SUB), bf16),
            pltpu.VMEM((M, SLOT_DEV), jnp.int32),
            pltpu.VMEM((2 * D, LANES), f32),
            pltpu.VMEM((D, SLOT_DEV), bf16),
            pltpu.VMEM((D, Q_DEV), bf16),
            pltpu.VMEM((D, Q_DEV), bf16),
            pltpu.VMEM((D, SLOT_DEV), f32),
            pltpu.VMEM((8, Q_DEV), f32),
            pltpu.VMEM((NEAR, 8, Q_DEV), f32),
            pltpu.VMEM((nz, 8, Q_DEV), f32),
            pltpu.VMEM((8, Q_DEV), f32),
            pltpu.VMEM((D, K), f32),
            pltpu.VMEM((Q_DEV, SLOT_DEV), bf16),
            pltpu.VMEM((D, 2 * Q_DEV), f32),
            pltpu.VMEM((M * Q_DEV, K), bf16),
            pltpu.VMEM((D, K), f32),
            pltpu.VMEM((D, Q_DEV), f32),
            pltpu.VMEM((NX, HEAD_ROWS, Q_DEV), bf16),
            pltpu.VMEM((D // 16, 2, 16, Q_DEV), bf16),
            pltpu.VMEM((HALF // 16, 2, 16, Q_DEV), bf16),
            pltpu.VMEM((NY, TILES, 2, 16, Q_DEV), bf16),
            pltpu.VMEM((NY, TILES, 2, 16, Q_DEV), bf16),
            pltpu.VMEM((TILES, 2, 16, Q_DEV), bf16),
            pltpu.VMEM((per, nz, 2, 16, Q_DEV), bf16),
            pltpu.VMEM((per, 16, Q_DEV), bf16),
            pltpu.VMEM((NX, 2, NY, G_ROWS, Q_DEV), bf16),
            pltpu.VMEM((NX, NY * C_ROWS, K), f32),
            pltpu.VMEM((CHIPS, 2 * C_ROWS, LANES), f32),
            pltpu.VMEM((2 * CHIPS, C_ROWS, LANES), f32),
            pltpu.VMEM((C_ROWS, LANES), f32),
            pltpu.VMEM((nz // 2, C_ROWS, LANES), f32),
            pltpu.VMEM((2 * D, LANES), f32),
            dma((5,)),
            dma((2, NEAR)),
            dma((2, nz)),
            dma((2, NX)),
            dma((2,)),
            dma((2, NY)),
            dma((TILES,)),
            dma((per, nz)),
            dma((per, nz)),
            dma((TILES,)),
            dma((2, CHIPS)),
            dma((2, NX)),
            dma((2, NX)),
            dma((2, 2 * CHIPS)),
            dma((2, nz // 2)),
            dma((2, 2 * CHIPS)),
            dma((2, NX)),
        ],
        compiler_params=pltpu.CompilerParams(
            collective_id=0, has_side_effects=True, vmem_limit_bytes=VMEM_BYTES
        ),
    )(slab_sizes, *ins)
    loss, head_grad, book = pl.pallas_call(
        finish_kernel,
        out_shape=[jax.ShapeDtypeStruct(shape, f32) for shape in outs],
        in_specs=[whole] * 3,
        out_specs=[left] * 3,
        scratch_shapes=[dma((6,))],
        compiler_params=pltpu.CompilerParams(vmem_limit_bytes=VMEM_BYTES),
    )(loss, head_grad, book)
    return loss.reshape(Q_DEV), head_grad, book


def solution(mesh):
    nz = mesh.shape["corpus"] // (2 * NY)
    return jax.shard_map(
        functools.partial(step, nz),
        mesh=mesh,
        in_specs=(P("query", None), P(), P(), P("corpus", None), P("corpus"), P("query")),
        out_specs=(P("query"), P("query", None), P()),
        check_vma=False,
    )
```
